128 devices in a mesh: fibre: 16 (over x, z_hi, core), tm: 8 (over y, z_lo).
Axes of the slice: x: 4, y: 4, z: 4 (z_hi: 2, z_lo: 2; z = z_hi * 2 + z_lo), core: 2. Of those that a mesh axis runs over, the one named last changes fastest.
Arguments:
- samples: bfloat16 [65536, 8192], P('tm', 'fibre'), may hold values from -6 to 6
- filter_taps: float32 [16, 512], replicated, may hold values from -1.5 to 1.5
- steering: bfloat16 [128, 2, 128, 1024], P('tm'), may hold values from -0.1875 to 0.1875
Outputs:
- beam_power: float32 [32, 128, 128, 128], P('fibre', 'tm')
The draws below stay inside these ranges and needn't reach their ends.
All inputs are finite; a program needn't handle non-finite values.
Results may differ from the reference program's by a relative error of at most 0.0052.
Values may be sent and summed in bfloat16 or wider, within the bound.
A program may use at most 704 MiB of HBM per device.

```python
import math
import jax
import jax.numpy as jnp
from jax import lax

NFFT = 512
TAPS = 16
KB = 128
KLO = 64
SLOW = 128
APER = 1024
STRIDE = 256
HALO = 384
CH_DEV = 512
CHANNELS = 8192
FRAMES = 128
SAMPLES_T = 65536
NAPERT = 32
N_FIBRE = 16


def level_of(own_key, extent, split, least, high):
    loudness = 1.0
    for position, parts in split:
        heights = jax.random.uniform(jax.random.fold_in(jax.random.fold_in(own_key, 6), position), (parts,), jnp.float32, least / len(split), high / len(split))
        loudness = loudness * jnp.repeat(jnp.exp(heights), extent[position] // parts).reshape((-1,) + (1,) * (len(extent) - 1 - position))
    return loudness


def normal_values(key, dims, deviation, bound, split=(), kind=jnp.bfloat16):
    gain = level_of(key, dims, split, -0.22, 0.18) if split else 1.0
    array = jax.random.normal(key, dims, jnp.float32) * deviation * gain
    return jnp.minimum(jnp.maximum(array, -bound), bound).astype(kind)


def setup_inputs(seed: int = 0) -> dict:
    streams_of = jax.random.split(jax.random.key(seed), 4)
    return {
        "samples": normal_values(streams_of[0], (SAMPLES_T, CHANNELS), 1.0, 6.0, ((0, 8), (1, 16))),
        "filter_taps": normal_values(streams_of[1], (TAPS, NFFT), TAPS ** -0.5, 1.5, (), jnp.float32),
        "steering": normal_values(streams_of[2], (KB, 2, SLOW, APER), APER ** -0.5, 0.1875, ((0, 8),)),
    }


def dft_table():
    sample_index = jnp.arange(NFFT, dtype=jnp.int32)
    bin_index = jnp.arange(KB, dtype=jnp.int32) + KLO
    phases = (bin_index[:, None] * sample_index[None, :] % NFFT).astype(jnp.float32) * (2.0 * math.pi / NFFT)
    fourier = jnp.concatenate([jnp.cos(phases), -jnp.sin(phases)], 0) / math.sqrt(NFFT)
    return fourier.astype(jnp.bfloat16)

def filterbank(longer, filter_taps, fourier):
    channels = longer.shape[1]
    count_frames = longer.shape[0] // NFFT - (TAPS - 1)
    framed = longer.reshape(count_frames + TAPS - 1, NFFT, channels)
    filtered = jnp.zeros((count_frames, NFFT, channels), jnp.float32)
    for tap_index in range(TAPS):
        offset = TAPS - 1 - tap_index
        filtered = filtered + filter_taps[tap_index][None, :, None] * framed[offset:offset + count_frames].astype(jnp.float32)
    filtered = filtered.astype(jnp.bfloat16)
    spectra = jnp.einsum('kn,fnc->fkc', fourier.astype(jnp.float32), filtered.astype(jnp.float32))
    return spectra.astype(jnp.bfloat16).reshape(count_frames, 2, KB, channels)

def reference(samples, filter_taps, steering):
    fourier = dft_table()

    def block_spectra(index):
        columns = lax.dynamic_slice_in_dim(samples, index * CH_DEV, CH_DEV, 1)
        lead_zeros = jnp.zeros(((TAPS - 1) * NFFT, CH_DEV), samples.dtype)
        return filterbank(jnp.concatenate([lead_zeros, columns], 0), filter_taps, fourier)
    stacked = lax.map(block_spectra, jnp.arange(N_FIBRE, dtype=jnp.int32))
    spectra = jnp.transpose(stacked, (1, 2, 3, 0, 4)).reshape(FRAMES, 2, KB, CHANNELS)
    edge_zeros = jnp.zeros((FRAMES, 2, KB, HALO), spectra.dtype)
    widened = jnp.concatenate([edge_zeros, spectra, edge_zeros], 3)
    weights = steering.astype(jnp.float32)

    def aperture_power(index):
        window = lax.dynamic_slice_in_dim(widened, index * STRIDE, APER, 3).astype(jnp.float32)
        products = jnp.einsum('fpkc,kqsc->kfpqs', window, weights)
        real_part = products[:, :, 0, 0, :] - products[:, :, 1, 1, :]
        imag_part = products[:, :, 1, 0, :] + products[:, :, 0, 1, :]
        return real_part * real_part + imag_part * imag_part
    return lax.map(aperture_power, jnp.arange(NAPERT, dtype=jnp.int32))
```

```python
import math

import jax
import jax.numpy as jnp
from jax import lax
from jax.experimental import pallas as pl
from jax.experimental.pallas import tpu as pltpu
from jax.sharding import PartitionSpec as P

NFFT = 512
TAPS = 16
KB = 128
KLO = 64
APER = 1024
FRAMES = 128
SLOW = 128

BLOCK = 16
SPAN = 31
CHUNK = 128
CHUNKS = 4
TM = 8
BINS = 16

MESH = pl.DeviceIdType.MESH
f32 = jnp.float32
bf16 = jnp.bfloat16

OFFSETS = ((0, 1), (1, 0), (3, 0), (2, 1), (1, 1), (2, 0), (3, 1))


def dft_table():
    sample_index = jnp.arange(NFFT, dtype=jnp.int32)
    bin_index = jnp.arange(KB, dtype=jnp.int32) + KLO
    phases = (bin_index[:, None] * sample_index[None, :] % NFFT).astype(f32) * (
        2.0 * math.pi / NFFT
    )
    fourier = jnp.stack([jnp.cos(phases), -jnp.sin(phases)], 0) / math.sqrt(NFFT)
    fourier = fourier.reshape(2, TM, BINS, NFFT).transpose(1, 0, 2, 3)
    return fourier.reshape(2 * KB, NFFT).astype(bf16)


def shifted(tm, dy, flip, sign):
    y, lo = tm // 2, tm % 2
    y = lax.rem(y + (dy if sign > 0 else 4 - dy), 4)
    return 2 * y + (1 - lo if flip else lo)


def kernel(
    x_ref, taps_ref, fourier_ref, steer_ref, out_ref,
    xb, wide, filt, send, recv, steer, spec, off_out, off_in, on_out, on_in,
    x_sem, steer_sem, own_sem, send_sem, recv_sem, off_ssem, off_rsem, on_ssem, on_rsem,
):
    tm = lax.axis_index("tm")
    fibre = lax.axis_index("fibre")
    core = fibre % 2
    count = 16
    partner = fibre + 1 - 2 * core
    outer = lax.rem(fibre + count - 1 + 2 * core, count)

    def there(tm_index, fibre_index):
        return {"fibre": fibre_index, "tm": tm_index}

    def chunk_of(step):
        return jnp.where(core == 0, step, CHUNKS - 1 - step)

    def x_copy(step):
        column = pl.multiple_of(chunk_of(step) * CHUNK, CHUNK)
        slot = step % 2
        return pltpu.make_async_copy(
            x_ref.at[:, :, pl.ds(column, CHUNK)], xb.at[slot], x_sem.at[slot]
        )

    steer_copy = pltpu.make_async_copy(steer_ref, steer, steer_sem)

    x_copy(0).start()
    steer_copy.start()

    barrier = pltpu.get_barrier_semaphore()
    for dy, flip in OFFSETS:
        pl.semaphore_signal(
            barrier, inc=1, device_id=there(shifted(tm, dy, flip, 1), fibre), device_id_type=MESH
        )
    for other in (partner, outer):
        pl.semaphore_signal(barrier, inc=1, device_id=there(tm, other), device_id_type=MESH)

    wide[...] = jnp.broadcast_to(taps_ref[...][:, :, None], (TAPS, NFFT, CHUNK))
    filt[:, SPAN * CHUNK :] = jnp.zeros((NFFT, CHUNK), bf16)
    recv[:, :, SPAN:] = jnp.zeros((CHUNKS, TM, 1, 2 * BINS, CHUNK), bf16)

    def to_peer(step, index):
        dy, flip = OFFSETS[index]
        target = shifted(tm, dy, flip, 1)
        return pltpu.make_async_remote_copy(
            src_ref=send.at[step, target, pl.ds(0, SPAN)],
            dst_ref=recv.at[step, tm, pl.ds(0, SPAN)],
            send_sem=send_sem.at[step, index],
            recv_sem=recv_sem.at[step, index],
            device_id=there(target, fibre),
            device_id_type=MESH,
        )

    def from_peer(step, index):
        dy, flip = OFFSETS[index]
        source = shifted(tm, dy, flip, -1)
        return pltpu.make_async_remote_copy(
            src_ref=send.at[step, source, pl.ds(0, SPAN)],
            dst_ref=recv.at[step, source, pl.ds(0, SPAN)],
            send_sem=send_sem.at[step, index],
            recv_sem=recv_sem.at[step, index],
            device_id=there(source, fibre),
            device_id_type=MESH,
        )

    def own_copy(step):
        return pltpu.make_async_copy(
            send.at[step, tm, pl.ds(0, SPAN)], recv.at[step, tm, pl.ds(0, SPAN)], own_sem.at[step]
        )

    def halo(out, landing, ssem, rsem, aperture, other):
        return pltpu.make_async_remote_copy(
            src_ref=out.at[aperture],
            dst_ref=landing.at[aperture],
            send_sem=ssem.at[aperture],
            recv_sem=rsem.at[aperture],
            device_id=there(tm, other),
            device_id_type=MESH,
        )

    def off_copy(aperture):
        return halo(off_out, off_in, off_ssem, off_rsem, aperture, outer)

    def on_copy(aperture):
        return halo(on_out, on_in, on_ssem, on_rsem, aperture, partner)

    def produce(step, carry):
        slot = step % 2
        x_copy(step).wait()

        @pl.when(step < CHUNKS - 1)
        def _():
            x_copy(step + 1).start()

        def filter_rows(index, carry):
            rows = pl.ds(pl.multiple_of(index * 16, 16), 16)
            xs = [xb[slot, g, rows, :].astype(f32) for g in range(BLOCK)]
            ts = [wide[t, rows, :] for t in range(TAPS)]
            for frame in range(SPAN):
                first, last = max(0, frame - BLOCK + 1), min(TAPS - 1, frame)
                total = ts[first] * xs[frame - first]
                for t in range(first + 1, last + 1):
                    total = total + ts[t] * xs[frame - t]
                filt[rows, frame * CHUNK : (frame + 1) * CHUNK] = total.astype(bf16)
            return carry

        lax.fori_loop(0, NFFT // 16, filter_rows, 0)

        def transform(pair, carry):
            columns = pl.ds(pl.multiple_of(pair * 2 * CHUNK, 2 * CHUNK), 2 * CHUNK)
            values = jnp.dot(
                fourier_ref[...], filt[:, columns], preferred_element_type=f32
            ).astype(bf16)
            for half in range(2):
                for d in range(TM):
                    send[step, d, pair * 2 + half] = values[
                        d * 2 * BINS : (d + 1) * 2 * BINS, half * CHUNK : (half + 1) * CHUNK
                    ]
            return carry

        lax.fori_loop(0, (SPAN + 1) // 2, transform, 0)

        @pl.when(step == 0)
        def _():
            pl.semaphore_wait(barrier, len(OFFSETS) + 2)

        for index in range(len(OFFSETS)):
            to_peer(step, index).start()
        own_copy(step).start()
        return carry

    lax.fori_loop(0, CHUNKS, produce, 0)

    def combine(step):
        for index in range(len(OFFSETS)):
            from_peer(step, index).wait_recv()
        own_copy(step).wait()
        columns = pl.ds(pl.multiple_of(chunk_of(step) * CHUNK, CHUNK), CHUNK)

        def block(i, carry):
            before = jnp.maximum(i - 1, 0)
            late = recv[step, before, pl.ds(BLOCK, BLOCK)].astype(f32)
            total = recv[step, i, pl.ds(0, BLOCK)].astype(f32) + jnp.where(i > 0, late, 0.0)
            turned = jnp.transpose(total, (1, 0, 2)).astype(bf16)
            for p in range(2):
                rows = pl.ds(pl.multiple_of(p * FRAMES + i * BLOCK, BLOCK), BLOCK)
                spec[:, rows, columns] = turned[p * BINS : (p + 1) * BINS]
            return carry

        lax.fori_loop(0, TM, block, 0)

    def product(k, u, width, m):
        if not isinstance(u, int):
            u, m = pl.multiple_of(u, CHUNK), pl.multiple_of(m, CHUNK)
        left = spec[k, :, pl.ds(u, width)]
        right = steer[k, :, pl.ds(m, width)]
        values = lax.dot_general(
            left, right, (((1,), (1,)), ((), ())), preferred_element_type=f32
        )
        real = values[:FRAMES, :SLOW] - values[FRAMES:, SLOW:]
        imag = values[FRAMES:, :SLOW] + values[:FRAMES, SLOW:]
        return real, imag

    def near(to_left, width):
        u = jnp.where(to_left, 0, 512 - width)
        m = jnp.where(to_left, APER - width, 0)
        return u, m

    def side(out, aperture, to_left, width):
        u, m = near(to_left, width)

        def one(k, carry):
            real, imag = product(k, u, width, m)
            out[aperture, k, 0] = real.astype(bf16)
            out[aperture, k, 1] = imag.astype(bf16)
            return carry

        lax.fori_loop(0, BINS, one, 0)

    combine(0)
    steer_copy.wait()
    side(off_out, core, core == 0, 128)
    off_copy(core).start()
    combine(1)
    combine(2)
    side(off_out, 1 - core, core == 0, 384)
    off_copy(1 - core).start()
    combine(3)
    side(on_out, 1 - core, core == 1, 128)
    on_copy(1 - core).start()
    side(on_out, core, core == 1, 384)
    on_copy(core).start()

    def own(k, carry):
        for aperture in range(2):
            real, imag = product(k, 0, 512, 384 - 256 * aperture)
            wide[k, pl.ds(aperture * 256, 128)] = real
            wide[k, pl.ds(aperture * 256 + 128, 128)] = imag
        return carry

    lax.fori_loop(0, BINS, own, 0)

    for aperture in range(2):
        on_copy(aperture).wait()
        off_copy(aperture).wait()
    inside = jnp.logical_and(
        jnp.logical_or(fibre > 0, core == 1), jnp.logical_or(fibre < count - 1, core == 0)
    )

    def finish(k, carry):
        for aperture in range(2):
            parts = []
            for part in range(2):
                total = wide[k, pl.ds(aperture * 256 + part * 128, 128)]
                total = total + on_in[aperture, k, part].astype(f32)
                total = total + jnp.where(inside, off_in[aperture, k, part].astype(f32), 0.0)
                parts.append(total)
            out_ref[aperture, k] = parts[0] * parts[0] + parts[1] * parts[1]
        return carry

    lax.fori_loop(0, BINS, finish, 0)

    def drain(step, carry):
        for index in range(len(OFFSETS)):
            to_peer(step, index).wait_send()
        return carry

    lax.fori_loop(0, CHUNKS, drain, 0)


def body(samples, filter_taps, steering):
    peers = len(OFFSETS)
    vmem = pl.BlockSpec(memory_space=pltpu.VMEM)
    hbm = pl.BlockSpec(memory_space=pl.ANY)
    dma = pltpu.SemaphoreType.DMA
    return pl.pallas_call(
        kernel,
        out_shape=jax.ShapeDtypeStruct((2, BINS, FRAMES, SLOW), f32),
        in_specs=[hbm, vmem, vmem, hbm],
        out_specs=vmem,
        scratch_shapes=[
            pltpu.VMEM((2, BLOCK, NFFT, CHUNK), bf16),
            pltpu.VMEM((TAPS, NFFT, CHUNK), f32),
            pltpu.VMEM((NFFT, (SPAN + 1) * CHUNK), bf16),
            pltpu.VMEM((CHUNKS, TM, SPAN + 1, 2 * BINS, CHUNK), bf16),
            pltpu.VMEM((CHUNKS, TM, SPAN + 1, 2 * BINS, CHUNK), bf16),
            pltpu.VMEM((BINS, 2 * SLOW, APER), bf16),
            pltpu.VMEM((BINS, 2 * FRAMES, CHUNKS * CHUNK), bf16),
            pltpu.VMEM((2, BINS, 2, FRAMES, SLOW), bf16),
            pltpu.VMEM((2, BINS, 2, FRAMES, SLOW), bf16),
            pltpu.VMEM((2, BINS, 2, FRAMES, SLOW), bf16),
            pltpu.VMEM((2, BINS, 2, FRAMES, SLOW), bf16),
            dma((2,)),
            dma,
            dma((CHUNKS,)),
            dma((CHUNKS, peers)),
            dma((CHUNKS, peers)),
            dma((2,)),
            dma((2,)),
            dma((2,)),
            dma((2,)),
        ],
        compiler_params=pltpu.CompilerParams(
            collective_id=0, has_side_effects=True, vmem_limit_bytes=60 * 2**20
        ),
        cost_estimate=pl.CostEstimate(
            flops=13 * 10**9, bytes_accessed=20 * 2**20, transcendentals=0
        ),
    )(
        samples.reshape(BLOCK, NFFT, samples.shape[1]),
        filter_taps,
        dft_table(),
        steering.reshape(BINS, 2 * SLOW, APER),
    )


def solution(mesh):
    in_specs = (P("tm", "fibre"), P(), P("tm", None, None, None))
    out_specs = P("fibre", "tm", None, None)
    return jax.shard_map(body, mesh=mesh, in_specs=in_specs, out_specs=out_specs, check_vma=False)
```

```python
import math

import jax
import jax.numpy as jnp
import numpy as np
from jax import lax
from jax.experimental import pallas as pl
from jax.experimental.pallas import tpu as pltpu
from jax.sharding import PartitionSpec as P

NFFT = 512
TAPS = 16
KB = 128
KLO = 64
APER = 1024
FRAMES = 128
SLOW = 128

BLOCK = 16
SPAN = 31
CHUNK = 128
CHUNKS = 4
TM = 8
BINS = 16
HALF = 8

MESH = pl.DeviceIdType.MESH
f32 = jnp.float32
bf16 = jnp.bfloat16

OFFSETS = ((0, 1), (1, 0), (3, 0), (2, 1), (1, 1), (2, 0), (3, 1))


def dft_table():
    sample_index = np.arange(NFFT, dtype=np.int32)
    bin_index = np.arange(KB, dtype=np.int32) + KLO
    phases = (bin_index[:, None] * sample_index[None, :] % NFFT).astype(np.float32)
    phases = phases * np.float32(2.0 * math.pi / NFFT)
    fourier = np.stack([np.cos(phases), -np.sin(phases)], 0) / np.float32(math.sqrt(NFFT))
    fourier = fourier.reshape(2, TM, 2, HALF, NFFT).transpose(1, 2, 0, 3, 4)
    return jnp.asarray(fourier.reshape(2 * KB, NFFT), bf16)


def shifted(tm, dy, flip, sign):
    y, lo = tm // 2, tm % 2
    y = lax.rem(y + (dy if sign > 0 else 4 - dy), 4)
    return 2 * y + (1 - lo if flip else lo)


def kernel(
    x_ref, taps_ref, fourier_ref, steer_ref, out_ref,
    xb, wide, filt, send, recv, steer, spec, off_out, off_in, on_out, on_in, back_out, back_in,
    x_sem, steer_sem, own_sem, send_sem, recv_sem, off_ssem, off_rsem, on_ssem, on_rsem, back_sem,
):
    tm = lax.axis_index("tm")
    fibre = lax.axis_index("fibre")
    core = fibre % 2
    hi = (fibre // 2) % 2
    count = 16
    flipped = tm + 1 - 2 * (tm % 2)
    partner = fibre + 1 - 2 * core
    outer = lax.rem(fibre + count - 1 + 2 * core, count)
    across = fibre + 2 - 4 * hi

    def there(tm_index, fibre_index):
        return {"fibre": fibre_index, "tm": tm_index}

    def chunk_of(step):
        return jnp.where(core == 0, step, CHUNKS - 1 - step)

    def x_copy(step):
        column = pl.multiple_of(chunk_of(step) * CHUNK, CHUNK)
        slot = step % 2
        return pltpu.make_async_copy(
            x_ref.at[:, :, pl.ds(column, CHUNK)], xb.at[slot], x_sem.at[slot]
        )

    quarter = HALF // 2
    steer_copy = pltpu.make_async_copy(
        steer_ref.at[pl.ds(hi * HALF, HALF)], steer.at[pl.ds(0, HALF)], steer_sem.at[0]
    )
    steer_swap = pltpu.make_async_remote_copy(
        src_ref=steer_ref.at[pl.ds(hi * HALF + core * quarter, quarter)],
        dst_ref=steer.at[pl.ds(HALF + core * quarter, quarter)],
        send_sem=steer_sem.at[1],
        recv_sem=steer_sem.at[2],
        device_id=there(flipped, across),
        device_id_type=MESH,
    )

    def steer_share(who):
        part = steer.at[pl.ds(HALF + who * quarter, quarter)]
        return pltpu.make_async_remote_copy(
            src_ref=part,
            dst_ref=part,
            send_sem=steer_sem.at[3],
            recv_sem=steer_sem.at[4],
            device_id=there(tm, partner),
            device_id_type=MESH,
        )

    x_copy(0).start()
    steer_copy.start()

    barrier = pltpu.get_barrier_semaphore()
    for dy, flip in OFFSETS:
        pl.semaphore_signal(
            barrier, inc=1, device_id=there(shifted(tm, dy, flip, 1), fibre), device_id_type=MESH
        )
    for other in (there(tm, partner), there(flipped, outer), there(flipped, across)):
        pl.semaphore_signal(barrier, inc=1, device_id=other, device_id_type=MESH)

    wide[...] = jnp.broadcast_to(taps_ref[...][:, :, None], (TAPS, NFFT, CHUNK))
    filt[:, SPAN * CHUNK :] = jnp.zeros((NFFT, CHUNK), bf16)
    recv[:, :, :, SPAN:] = jnp.zeros((CHUNKS, 2, TM, 1, 2 * HALF, CHUNK), bf16)

    frames = pl.ds(0, SPAN)

    def to_peer(step, part, index):
        dy, flip = OFFSETS[index]
        target = shifted(tm, dy, flip, 1)
        return pltpu.make_async_remote_copy(
            src_ref=send.at[step, part, target, frames],
            dst_ref=recv.at[step, part, tm, frames],
            send_sem=send_sem.at[step, part, index],
            recv_sem=recv_sem.at[step, part, index],
            device_id=there(target, fibre),
            device_id_type=MESH,
        )

    def from_peer(step, part, index):
        dy, flip = OFFSETS[index]
        source = shifted(tm, dy, flip, -1)
        return pltpu.make_async_remote_copy(
            src_ref=send.at[step, part, source, frames],
            dst_ref=recv.at[step, part, source, frames],
            send_sem=send_sem.at[step, part, index],
            recv_sem=recv_sem.at[step, part, index],
            device_id=there(source, fibre),
            device_id_type=MESH,
        )

    def own_copy(step, part):
        return pltpu.make_async_copy(
            send.at[step, part, tm, frames], recv.at[step, part, tm, frames], own_sem.at[step, part]
        )

    def send_all(step, part):
        for index in range(len(OFFSETS)):
            to_peer(step, part, index).start()
        own_copy(step, part).start()

    def off_copy(aperture, part, landing):
        return pltpu.make_async_remote_copy(
            src_ref=off_out.at[aperture, part],
            dst_ref=off_in.at[aperture, landing],
            send_sem=off_ssem.at[aperture, part],
            recv_sem=off_rsem.at[aperture, landing],
            device_id=there(flipped, outer),
            device_id_type=MESH,
        )

    def on_copy(aperture, part):
        return pltpu.make_async_remote_copy(
            src_ref=on_out.at[aperture, part],
            dst_ref=on_in.at[aperture, part],
            send_sem=on_ssem.at[aperture, part],
            recv_sem=on_rsem.at[aperture, part],
            device_id=there(tm, partner),
            device_id_type=MESH,
        )

    back_copy = pltpu.make_async_remote_copy(
        src_ref=back_out,
        dst_ref=back_in,
        send_sem=back_sem.at[0],
        recv_sem=back_sem.at[1],
        device_id=there(flipped, fibre),
        device_id_type=MESH,
    )

    parts = [jnp.where(hi == h, 0, 1) for h in range(2)]
    targets = [[jnp.where(hi == h, t, t + 1 - 2 * (t % 2)) for h in range(2)] for t in range(TM)]

    def produce(step, carry):
        slot = step % 2
        x_copy(step).wait()

        @pl.when(step < CHUNKS - 1)
        def _():
            x_copy(step + 1).start()

        def filter_rows(index, carry):
            rows = pl.ds(pl.multiple_of(index * 16, 16), 16)
            xs = [xb[slot, g, rows, :].astype(f32) for g in range(BLOCK)]
            ts = [wide[t, rows, :] for t in range(TAPS)]
            for frame in range(SPAN):
                first, last = max(0, frame - BLOCK + 1), min(TAPS - 1, frame)
                total = ts[first] * xs[frame - first]
                for t in range(first + 1, last + 1):
                    total = total + ts[t] * xs[frame - t]
                filt[rows, frame * CHUNK : (frame + 1) * CHUNK] = total.astype(bf16)
            return carry

        lax.fori_loop(0, NFFT // 16, filter_rows, 0)

        def transform(pair, carry):
            columns = pl.ds(pl.multiple_of(pair * 2 * CHUNK, 2 * CHUNK), 2 * CHUNK)
            values = jnp.dot(
                fourier_ref[...], filt[:, columns], preferred_element_type=f32
            ).astype(bf16)
            for side_frame in range(2):
                for t in range(TM):
                    for h in range(2):
                        row = (2 * t + h) * 2 * HALF
                        send[step, parts[h], targets[t][h], pair * 2 + side_frame] = values[
                            row : row + 2 * HALF, side_frame * CHUNK : (side_frame + 1) * CHUNK
                        ]
            return carry

        lax.fori_loop(0, (SPAN + 1) // 2, transform, 0)

        @pl.when(step == 0)
        def _():
            pl.semaphore_wait(barrier, len(OFFSETS) + 3)
            steer_swap.start()

        send_all(step, 1)

        @pl.when(step < 2)
        def _():
            send_all(step, 0)

        return carry

    lax.fori_loop(0, CHUNKS, produce, 0)
    send_all(2, 0)
    send_all(3, 0)

    def combine(step, part):
        for index in range(len(OFFSETS)):
            from_peer(step, part, index).wait_recv()
        own_copy(step, part).wait()
        columns = pl.ds(pl.multiple_of(chunk_of(step) * CHUNK, CHUNK), CHUNK)

        def block(i, carry):
            before = jnp.maximum(i - 1, 0)
            late = recv[step, part, before, pl.ds(BLOCK, BLOCK)].astype(f32)
            total = recv[step, part, i, pl.ds(0, BLOCK)].astype(f32) + jnp.where(i > 0, late, 0.0)
            turned = jnp.transpose(total, (1, 0, 2)).astype(bf16)
            for p in range(2):
                rows = pl.ds(pl.multiple_of(p * FRAMES + i * BLOCK, BLOCK), BLOCK)
                spec[pl.ds(part * HALF, HALF), rows, columns] = turned[p * HALF : (p + 1) * HALF]
            return carry

        lax.fori_loop(0, TM, block, 0)

    def product(k, u, width, m):
        if not isinstance(u, int):
            u, m = pl.multiple_of(u, CHUNK), pl.multiple_of(m, CHUNK)
        left = spec[k, :, pl.ds(u, width)]
        right = steer[k, :, pl.ds(m, width)]
        values = lax.dot_general(
            left, right, (((1,), (1,)), ((), ())), preferred_element_type=f32
        )
        real = values[:FRAMES, :SLOW] - values[FRAMES:, SLOW:]
        imag = values[FRAMES:, :SLOW] + values[:FRAMES, SLOW:]
        return real, imag

    def side(out, aperture, part, to_left, width):
        u = jnp.where(to_left, 0, 512 - width)
        m = jnp.where(to_left, APER - width, 0)

        def one(k, carry):
            real, imag = product(part * HALF + k, u, width, m)
            out[aperture, part, k, 0] = real.astype(bf16)
            out[aperture, part, k, 1] = imag.astype(bf16)
            return carry

        lax.fori_loop(0, HALF, one, 0)

    def off_near(part):
        side(off_out, core, part, core == 0, 128)
        off_copy(core, part, 1 - part).start()

    def off_far(part):
        side(off_out, 1 - core, part, core == 0, 384)
        off_copy(1 - core, part, 1 - part).start()

    def on_chip(part):
        side(on_out, 1 - core, part, core == 1, 128)
        on_copy(1 - core, part).start()
        side(on_out, core, part, core == 1, 384)
        on_copy(core, part).start()

    def own(part):
        def one(k, carry):
            k = part * HALF + k
            for aperture in range(2):
                real, imag = product(k, 0, 512, 384 - 256 * aperture)
                wide[k, pl.ds(aperture * 256, 128)] = real
                wide[k, pl.ds(aperture * 256 + 128, 128)] = imag
            return carry

        lax.fori_loop(0, HALF, one, 0)

    inside = jnp.logical_and(
        jnp.logical_or(fibre > 0, core == 1), jnp.logical_or(fibre < count - 1, core == 0)
    )

    def power(part, aperture, k):
        squares = []
        for piece in range(2):
            total = wide[part * HALF + k, pl.ds(aperture * 256 + piece * 128, 128)]
            total = total + on_in[aperture, part, k, piece].astype(f32)
            far = off_in[aperture, part, k, piece].astype(f32)
            total = total + jnp.where(inside, far, 0.0)
            squares.append(total * total)
        return squares[0] + squares[1]

    def wait_sides(part):
        for aperture in range(2):
            on_copy(aperture, part).wait_recv()
            off_copy(aperture, 1 - part, part).wait_recv()

    combine(0, 1)
    combine(0, 0)
    steer_copy.wait()
    off_near(0)
    steer_swap.wait()
    steer_share(core).start()
    combine(1, 1)
    combine(1, 0)
    steer_share(1 - core).wait_recv()
    off_near(1)
    combine(2, 1)
    off_far(1)
    combine(3, 1)
    on_chip(1)
    own(1)
    combine(2, 0)
    off_far(0)
    wait_sides(1)

    def finish_other(k, carry):
        for aperture in range(2):
            back_out[aperture, k] = power(1, aperture, k).astype(bf16)
        return carry

    lax.fori_loop(0, HALF, finish_other, 0)
    back_copy.start()

    combine(3, 0)
    on_chip(0)
    own(0)
    wait_sides(0)

    def finish_own(k, carry):
        for aperture in range(2):
            out_ref[aperture, hi * HALF + k] = power(0, aperture, k)
        return carry

    lax.fori_loop(0, HALF, finish_own, 0)

    back_copy.wait()

    def place(k, carry):
        for aperture in range(2):
            out_ref[aperture, (1 - hi) * HALF + k] = back_in[aperture, k].astype(f32)
        return carry

    lax.fori_loop(0, HALF, place, 0)

    steer_share(core).wait_send()
    for part in range(2):
        for aperture in range(2):
            on_copy(aperture, part).wait_send()
            off_copy(aperture, part, 1 - part).wait_send()

    def drain(step, carry):
        for part in range(2):
            for index in range(len(OFFSETS)):
                to_peer(step, part, index).wait_send()
        return carry

    lax.fori_loop(0, CHUNKS, drain, 0)


def body(samples, filter_taps, steering):
    peers = len(OFFSETS)
    vmem = pl.BlockSpec(memory_space=pltpu.VMEM)
    hbm = pl.BlockSpec(memory_space=pl.ANY)
    dma = pltpu.SemaphoreType.DMA
    return pl.pallas_call(
        kernel,
        out_shape=jax.ShapeDtypeStruct((2, BINS, FRAMES, SLOW), f32),
        in_specs=[hbm, vmem, vmem, hbm],
        out_specs=vmem,
        scratch_shapes=[
            pltpu.VMEM((2, BLOCK, NFFT, CHUNK), bf16),
            pltpu.VMEM((TAPS, NFFT, CHUNK), f32),
            pltpu.VMEM((NFFT, (SPAN + 1) * CHUNK), bf16),
            pltpu.VMEM((CHUNKS, 2, TM, SPAN + 1, 2 * HALF, CHUNK), bf16),
            pltpu.VMEM((CHUNKS, 2, TM, SPAN + 1, 2 * HALF, CHUNK), bf16),
            pltpu.VMEM((BINS, 2 * SLOW, APER), bf16),
            pltpu.VMEM((BINS, 2 * FRAMES, CHUNKS * CHUNK), bf16),
            pltpu.VMEM((2, 2, HALF, 2, FRAMES, SLOW), bf16),
            pltpu.VMEM((2, 2, HALF, 2, FRAMES, SLOW), bf16),
            pltpu.VMEM((2, 2, HALF, 2, FRAMES, SLOW), bf16),
            pltpu.VMEM((2, 2, HALF, 2, FRAMES, SLOW), bf16),
            pltpu.VMEM((2, HALF, FRAMES, SLOW), bf16),
            pltpu.VMEM((2, HALF, FRAMES, SLOW), bf16),
            dma((2,)),
            dma((5,)),
            dma((CHUNKS, 2)),
            dma((CHUNKS, 2, peers)),
            dma((CHUNKS, 2, peers)),
            dma((2, 2)),
            dma((2, 2)),
            dma((2, 2)),
            dma((2, 2)),
            dma((2,)),
        ],
        compiler_params=pltpu.CompilerParams(
            collective_id=0, has_side_effects=True, vmem_limit_bytes=60 * 2**20
        ),
        cost_estimate=pl.CostEstimate(
            flops=13 * 10**9, bytes_accessed=20 * 2**20, transcendentals=0
        ),
    )(
        samples.reshape(BLOCK, NFFT, samples.shape[1]),
        filter_taps,
        dft_table(),
        steering.reshape(BINS, 2 * SLOW, APER),
    )


def solution(mesh):
    in_specs = (P("tm", "fibre"), P(), P("tm", None, None, None))
    out_specs = P("fibre", "tm", None, None)
    return jax.shard_map(body, mesh=mesh, in_specs=in_specs, out_specs=out_specs, check_vma=False)
```

```python
import math

import jax
import jax.numpy as jnp
import numpy as np
from jax import lax
from jax.experimental import pallas as pl
from jax.experimental.pallas import tpu as pltpu
from jax.sharding import PartitionSpec as P

NFFT = 512
TAPS = 16
KB = 128
KLO = 64
APER = 1024
FRAMES = 128
SLOW = 128

BLOCK = 16
SPAN = 31
CHUNK = 128
CHUNKS = 4
TM = 8
BINS = 16
HALF = 8
GROUPS = ((0, 8), (8, 16), (16, 24), (24, 31))

MESH = pl.DeviceIdType.MESH
f32 = jnp.float32
bf16 = jnp.bfloat16

OFFSETS = ((0, 1), (1, 0), (3, 0), (2, 1), (1, 1), (2, 0), (3, 1))


def dft_table():
    sample_index = np.arange(NFFT, dtype=np.int32)
    bin_index = np.arange(KB, dtype=np.int32) + KLO
    phases = (bin_index[:, None] * sample_index[None, :] % NFFT).astype(np.float32)
    phases = phases * np.float32(2.0 * math.pi / NFFT)
    fourier = np.stack([np.cos(phases), -np.sin(phases)], 0) / np.float32(math.sqrt(NFFT))
    fourier = fourier.reshape(2, TM, 2, HALF, NFFT).transpose(1, 2, 0, 3, 4)
    return jnp.asarray(fourier.reshape(2 * KB, NFFT), bf16)


def peer(tm, core, index, sign):
    (dy0, flip0), (dy1, flip1) = OFFSETS[index], OFFSETS[len(OFFSETS) - 1 - index]
    dy, flip = jnp.where(core == 0, dy0, dy1), jnp.where(core == 0, flip0, flip1)
    lo = tm % 2
    y = lax.rem(tm // 2 + (dy if sign > 0 else 4 - dy), 4)
    return 2 * y + lo + flip - 2 * lo * flip


def kernel(
    x_ref, taps_ref, fourier_ref, steer_ref, out_ref,
    xb, wide, filt, send, recv, steer, spec, off_out, off_in, on_out, on_in, back_out, back_in,
    x_sem, steer_sem, own_sem, send_sem, recv_sem, off_ssem, off_rsem, on_ssem, on_rsem, back_sem,
):
    tm = lax.axis_index("tm")
    fibre = lax.axis_index("fibre")
    core = fibre % 2
    hi = (fibre // 2) % 2
    count = 16
    flipped = tm + 1 - 2 * (tm % 2)
    partner = fibre + 1 - 2 * core
    outer = lax.rem(fibre + count - 1 + 2 * core, count)
    across = fibre + 2 - 4 * hi

    def there(tm_index, fibre_index):
        return {"fibre": fibre_index, "tm": tm_index}

    def chunk_of(step):
        return jnp.where(core == 0, step, CHUNKS - 1 - step)

    def x_copy(step):
        column = pl.multiple_of(chunk_of(step) * CHUNK, CHUNK)
        slot = step % 2
        return pltpu.make_async_copy(
            x_ref.at[:, :, pl.ds(column, CHUNK)], xb.at[slot], x_sem.at[slot]
        )

    def x_first(number):
        column = pl.multiple_of(chunk_of(0) * CHUNK, CHUNK)
        some = pl.ds(number * (BLOCK // 2), BLOCK // 2)
        return pltpu.make_async_copy(
            x_ref.at[some, :, pl.ds(column, CHUNK)], xb.at[0, some], x_sem.at[2 * number]
        )

    quarter = HALF // 2
    steer_copy = pltpu.make_async_copy(
        steer_ref.at[pl.ds(hi * HALF, HALF)], steer.at[pl.ds(0, HALF)], steer_sem.at[0]
    )
    steer_swap = pltpu.make_async_remote_copy(
        src_ref=steer_ref.at[pl.ds(hi * HALF + core * quarter, quarter)],
        dst_ref=steer.at[pl.ds(HALF + core * quarter, quarter)],
        send_sem=steer_sem.at[1],
        recv_sem=steer_sem.at[2],
        device_id=there(flipped, across),
        device_id_type=MESH,
    )

    def steer_share(who):
        part = steer.at[pl.ds(HALF + who * quarter, quarter)]
        return pltpu.make_async_remote_copy(
            src_ref=part,
            dst_ref=part,
            send_sem=steer_sem.at[3],
            recv_sem=steer_sem.at[4],
            device_id=there(tm, partner),
            device_id_type=MESH,
        )

    x_first(0).start()
    x_first(1).start()
    steer_copy.start()

    barrier = pltpu.get_barrier_semaphore()
    for index in range(len(OFFSETS)):
        pl.semaphore_signal(
            barrier, inc=1, device_id=there(peer(tm, core, index, 1), fibre), device_id_type=MESH
        )
    for other in (there(tm, partner), there(flipped, outer), there(flipped, across)):
        pl.semaphore_signal(barrier, inc=1, device_id=other, device_id_type=MESH)

    wide[...] = jnp.broadcast_to(taps_ref[...][:, :, None], (TAPS, NFFT, CHUNK))
    filt[:, SPAN * CHUNK :] = jnp.zeros((NFFT, CHUNK), bf16)
    recv[:, :, :, SPAN:] = jnp.zeros((CHUNKS, TM, 2, 1, 2 * HALF, CHUNK), bf16)

    whole = (0, SPAN)

    def piece(ref, step, device, part, frames):
        sets = pl.ds(0, 2) if part is None else pl.ds(part, 1)
        return ref.at[step, device, sets, pl.ds(frames[0], frames[1] - frames[0])]

    def to_peer(step, part, index, frames=whole):
        target = peer(tm, core, index, 1)
        slot = 0 if part is None else part
        return pltpu.make_async_remote_copy(
            src_ref=piece(send, step, target, part, frames),
            dst_ref=piece(recv, step, tm, part, frames),
            send_sem=send_sem.at[step, slot, index],
            recv_sem=recv_sem.at[step, slot, index],
            device_id=there(target, fibre),
            device_id_type=MESH,
        )

    def from_peer(step, part, index):
        source = peer(tm, core, index, -1)
        slot = 0 if part is None else part
        return pltpu.make_async_remote_copy(
            src_ref=piece(send, step, source, part, whole),
            dst_ref=piece(recv, step, source, part, whole),
            send_sem=send_sem.at[step, slot, index],
            recv_sem=recv_sem.at[step, slot, index],
            device_id=there(source, fibre),
            device_id_type=MESH,
        )

    def own_copy(step, part):
        return pltpu.make_async_copy(
            piece(send, step, tm, part, whole),
            piece(recv, step, tm, part, whole),
            own_sem.at[step, 0 if part is None else part],
        )

    def send_all(step, part):
        for index in range(len(OFFSETS)):
            to_peer(step, part, index).start()
        own_copy(step, part).start()

    def off_copy(aperture, part, landing):
        return pltpu.make_async_remote_copy(
            src_ref=off_out.at[aperture, part],
            dst_ref=off_in.at[aperture, landing],
            send_sem=off_ssem.at[aperture, part],
            recv_sem=off_rsem.at[aperture, landing],
            device_id=there(flipped, outer),
            device_id_type=MESH,
        )

    def on_copy(aperture, part):
        return pltpu.make_async_remote_copy(
            src_ref=on_out.at[aperture, part],
            dst_ref=on_in.at[aperture, part],
            send_sem=on_ssem.at[aperture, part],
            recv_sem=on_rsem.at[aperture, part],
            device_id=there(tm, partner),
            device_id_type=MESH,
        )

    back_copy = pltpu.make_async_remote_copy(
        src_ref=back_out,
        dst_ref=back_in,
        send_sem=back_sem.at[0],
        recv_sem=back_sem.at[1],
        device_id=there(flipped, fibre),
        device_id_type=MESH,
    )

    parts = [jnp.where(hi == h, 0, 1) for h in range(2)]
    targets = [[jnp.where(hi == h, t, t + 1 - 2 * (t % 2)) for h in range(2)] for t in range(TM)]

    def filter_frames(slot, frames):
        first_x, last_x = max(0, frames[0] - TAPS + 1), min(BLOCK, frames[1])

        def filter_rows(index, carry):
            rows = pl.ds(pl.multiple_of(index * 16, 16), 16)
            xs = {g: xb[slot, g, rows, :].astype(f32) for g in range(first_x, last_x)}
            ts = [wide[t, rows, :] for t in range(TAPS)]
            for frame in range(*frames):
                first, last = max(0, frame - BLOCK + 1), min(TAPS - 1, frame)
                total = ts[first] * xs[frame - first]
                for t in range(first + 1, last + 1):
                    total = total + ts[t] * xs[frame - t]
                filt[rows, frame * CHUNK : (frame + 1) * CHUNK] = total.astype(bf16)
            return carry

        lax.fori_loop(0, NFFT // 16, filter_rows, 0)

    def transform_frames(step, frames):
        def transform(pair, carry):
            columns = pl.ds(pl.multiple_of(pair * 2 * CHUNK, 2 * CHUNK), 2 * CHUNK)
            values = jnp.dot(
                fourier_ref[...], filt[:, columns], preferred_element_type=f32
            ).astype(bf16)
            for odd in range(2):
                for t in range(TM):
                    for h in range(2):
                        row = (2 * t + h) * 2 * HALF
                        send[step, targets[t][h], parts[h], pair * 2 + odd] = values[
                            row : row + 2 * HALF, odd * CHUNK : (odd + 1) * CHUNK
                        ]
            return carry

        lax.fori_loop(frames[0] // 2, (frames[1] + 1) // 2, transform, 0)

    for number, frames in enumerate(GROUPS):
        if number < 2:
            x_first(number).wait()
        if number == 1:
            x_copy(1).start()
        filter_frames(0, frames)
        transform_frames(0, frames)
        if number == 0:
            pl.semaphore_wait(barrier, len(OFFSETS) + 3)
        for index in range(len(OFFSETS)):
            to_peer(0, None, index, frames).start()
        if number == 0:
            steer_swap.start()
    own_copy(0, None).start()

    def produce(step, carry):
        x_copy(step).wait()

        @pl.when(step < CHUNKS - 1)
        def _():
            x_copy(step + 1).start()

        filter_frames(step % 2, whole)
        transform_frames(step, whole)

        @pl.when(step == 1)
        def _():
            send_all(1, None)

        @pl.when(step > 1)
        def _():
            send_all(step, 1)

        return carry

    lax.fori_loop(1, CHUNKS, produce, 0)
    send_all(2, 0)
    send_all(3, 0)

    def arrive(step, part):
        for index in range(len(OFFSETS)):
            from_peer(step, part, index).wait_recv()
        own_copy(step, part).wait()

    def combine(step, part):
        columns = pl.ds(pl.multiple_of(chunk_of(step) * CHUNK, CHUNK), CHUNK)

        def block(i, carry):
            before = jnp.maximum(i - 1, 0)
            late = recv[step, before, part, pl.ds(BLOCK, BLOCK)].astype(f32)
            total = recv[step, i, part, pl.ds(0, BLOCK)].astype(f32) + jnp.where(i > 0, late, 0.0)
            turned = jnp.transpose(total, (1, 0, 2)).astype(bf16)
            for p in range(2):
                rows = pl.ds(pl.multiple_of(p * FRAMES + i * BLOCK, BLOCK), BLOCK)
                spec[pl.ds(part * HALF, HALF), rows, columns] = turned[p * HALF : (p + 1) * HALF]
            return carry

        lax.fori_loop(0, TM, block, 0)

    def product(k, u, width, m):
        if not isinstance(u, int):
            u, m = pl.multiple_of(u, CHUNK), pl.multiple_of(m, CHUNK)
        left = spec[k, :, pl.ds(u, width)]
        right = steer[k, :, pl.ds(m, width)]
        values = lax.dot_general(
            left, right, (((1,), (1,)), ((), ())), preferred_element_type=f32
        )
        real = values[:FRAMES, :SLOW] - values[FRAMES:, SLOW:]
        imag = values[FRAMES:, :SLOW] + values[:FRAMES, SLOW:]
        return real, imag

    def side(out, aperture, part, to_left, width):
        u = jnp.where(to_left, 0, 512 - width)
        m = jnp.where(to_left, APER - width, 0)

        def one(k, carry):
            real, imag = product(part * HALF + k, u, width, m)
            out[aperture, part, k, 0] = real.astype(bf16)
            out[aperture, part, k, 1] = imag.astype(bf16)
            return carry

        lax.fori_loop(0, HALF, one, 0)

    def off_near(part):
        side(off_out, core, part, core == 0, 128)
        off_copy(core, part, 1 - part).start()

    def off_far(part):
        side(off_out, 1 - core, part, core == 0, 384)
        off_copy(1 - core, part, 1 - part).start()

    def on_chip(part):
        side(on_out, 1 - core, part, core == 1, 128)
        on_copy(1 - core, part).start()
        side(on_out, core, part, core == 1, 384)
        on_copy(core, part).start()

    def own(part):
        def one(k, carry):
            k = part * HALF + k
            for aperture in range(2):
                real, imag = product(k, 0, 512, 384 - 256 * aperture)
                wide[k, pl.ds(aperture * 256, 128)] = real
                wide[k, pl.ds(aperture * 256 + 128, 128)] = imag
            return carry

        lax.fori_loop(0, HALF, one, 0)

    inside = jnp.logical_and(
        jnp.logical_or(fibre > 0, core == 1), jnp.logical_or(fibre < count - 1, core == 0)
    )

    def power(part, aperture, k):
        squares = []
        for piece in range(2):
            total = wide[part * HALF + k, pl.ds(aperture * 256 + piece * 128, 128)]
            total = total + on_in[aperture, part, k, piece].astype(f32)
            far = off_in[aperture, part, k, piece].astype(f32)
            total = total + jnp.where(inside, far, 0.0)
            squares.append(total * total)
        return squares[0] + squares[1]

    def wait_sides(part):
        for aperture in range(2):
            on_copy(aperture, part).wait_recv()
            off_copy(aperture, 1 - part, part).wait_recv()

    arrive(0, None)
    combine(0, 0)
    steer_copy.wait()
    off_near(0)
    combine(0, 1)
    steer_swap.wait()
    steer_share(core).start()
    arrive(1, None)
    combine(1, 1)
    combine(1, 0)
    steer_share(1 - core).wait_recv()
    off_near(1)
    arrive(2, 1)
    combine(2, 1)
    off_far(1)
    arrive(3, 1)
    combine(3, 1)
    on_chip(1)
    own(1)
    arrive(2, 0)
    combine(2, 0)
    off_far(0)
    wait_sides(1)

    def finish_other(k, carry):
        for aperture in range(2):
            back_out[aperture, k] = power(1, aperture, k).astype(bf16)
        return carry

    lax.fori_loop(0, HALF, finish_other, 0)
    back_copy.start()

    arrive(3, 0)
    combine(3, 0)
    on_chip(0)
    own(0)
    wait_sides(0)

    def finish_own(k, carry):
        for aperture in range(2):
            out_ref[aperture, hi * HALF + k] = power(0, aperture, k)
        return carry

    lax.fori_loop(0, HALF, finish_own, 0)

    back_copy.wait()

    def place(k, carry):
        for aperture in range(2):
            out_ref[aperture, (1 - hi) * HALF + k] = back_in[aperture, k].astype(f32)
        return carry

    lax.fori_loop(0, HALF, place, 0)

    steer_share(core).wait_send()
    for part in range(2):
        for aperture in range(2):
            on_copy(aperture, part).wait_send()
            off_copy(aperture, part, 1 - part).wait_send()

    def drain(index_of_parts, steps):
        def one(step, carry):
            for part in index_of_parts:
                for index in range(len(OFFSETS)):
                    to_peer(step, part, index).wait_send()
            return carry

        lax.fori_loop(*steps, one, 0)

    drain((None,), (0, 2))
    drain((0, 1), (2, CHUNKS))


def body(samples, filter_taps, steering):
    peers = len(OFFSETS)
    vmem = pl.BlockSpec(memory_space=pltpu.VMEM)
    hbm = pl.BlockSpec(memory_space=pl.ANY)
    dma = pltpu.SemaphoreType.DMA
    return pl.pallas_call(
        kernel,
        out_shape=jax.ShapeDtypeStruct((2, BINS, FRAMES, SLOW), f32),
        in_specs=[hbm, vmem, vmem, hbm],
        out_specs=vmem,
        scratch_shapes=[
            pltpu.VMEM((2, BLOCK, NFFT, CHUNK), bf16),
            pltpu.VMEM((TAPS, NFFT, CHUNK), f32),
            pltpu.VMEM((NFFT, (SPAN + 1) * CHUNK), bf16),
            pltpu.VMEM((CHUNKS, TM, 2, SPAN + 1, 2 * HALF, CHUNK), bf16),
            pltpu.VMEM((CHUNKS, TM, 2, SPAN + 1, 2 * HALF, CHUNK), bf16),
            pltpu.VMEM((BINS, 2 * SLOW, APER), bf16),
            pltpu.VMEM((BINS, 2 * FRAMES, CHUNKS * CHUNK), bf16),
            pltpu.VMEM((2, 2, HALF, 2, FRAMES, SLOW), bf16),
            pltpu.VMEM((2, 2, HALF, 2, FRAMES, SLOW), bf16),
            pltpu.VMEM((2, 2, HALF, 2, FRAMES, SLOW), bf16),
            pltpu.VMEM((2, 2, HALF, 2, FRAMES, SLOW), bf16),
            pltpu.VMEM((2, HALF, FRAMES, SLOW), bf16),
            pltpu.VMEM((2, HALF, FRAMES, SLOW), bf16),
            dma((3,)),
            dma((5,)),
            dma((CHUNKS, 2)),
            dma((CHUNKS, 2, peers)),
            dma((CHUNKS, 2, peers)),
            dma((2, 2)),
            dma((2, 2)),
            dma((2, 2)),
            dma((2, 2)),
            dma((2,)),
        ],
        compiler_params=pltpu.CompilerParams(
            collective_id=0, has_side_effects=True, vmem_limit_bytes=60 * 2**20
        ),
        cost_estimate=pl.CostEstimate(
            flops=13 * 10**9, bytes_accessed=20 * 2**20, transcendentals=0
        ),
    )(
        samples.reshape(BLOCK, NFFT, samples.shape[1]),
        filter_taps,
        dft_table(),
        steering.reshape(BINS, 2 * SLOW, APER),
    )


def solution(mesh):
    in_specs = (P("tm", "fibre"), P(), P("tm", None, None, None))
    out_specs = P("fibre", "tm", None, None)
    return jax.shard_map(body, mesh=mesh, in_specs=in_specs, out_specs=out_specs, check_vma=False)
```

```python
import math

import jax
import jax.numpy as jnp
import numpy as np
from jax import lax
from jax.experimental import pallas as pl
from jax.experimental.pallas import tpu as pltpu
from jax.sharding import PartitionSpec as P

NFFT = 512
TAPS = 16
KB = 128
KLO = 64
APER = 1024
FRAMES = 128
SLOW = 128

BLOCK = 16
SPAN = 31
CHUNK = 128
CHUNKS = 4
TM = 8
BINS = 16
HALF = 8
GROUPS = ((0, 4), (4, 8), (8, 16), (16, 24), (24, 31))

MESH = pl.DeviceIdType.MESH
f32 = jnp.float32
bf16 = jnp.bfloat16

OFFSETS = ((2, 1), (0, 1), (2, 0), (1, 1), (1, 0), (3, 1), (3, 0))
OFFSETS1 = ((3, 0), (3, 1), (1, 0), (1, 1), (2, 0), (0, 1), (2, 1))


def dft_table():
    sample_index = np.arange(NFFT, dtype=np.int32)
    bin_index = np.arange(KB, dtype=np.int32) + KLO
    phases = (bin_index[:, None] * sample_index[None, :] % NFFT).astype(np.float32)
    phases = phases * np.float32(2.0 * math.pi / NFFT)
    fourier = np.stack([np.cos(phases), -np.sin(phases)], 0) / np.float32(math.sqrt(NFFT))
    fourier = fourier.reshape(2, TM, 2, HALF, NFFT).transpose(1, 2, 0, 3, 4)
    return jnp.asarray(fourier.reshape(2 * KB, NFFT), bf16)


def peer(tm, core, index, sign):
    (dy0, flip0), (dy1, flip1) = OFFSETS[index], OFFSETS1[index]
    dy, flip = jnp.where(core == 0, dy0, dy1), jnp.where(core == 0, flip0, flip1)
    lo = tm % 2
    y = lax.rem(tm // 2 + (dy if sign > 0 else 4 - dy), 4)
    return 2 * y + lo + flip - 2 * lo * flip


def kernel(
    x_ref, taps_ref, fourier_ref, steer_ref, out_ref,
    xb, wide, filt, send, recv, steer, spec, off_out, off_in, on_out, on_in, back_out, back_in,
    x_sem, steer_sem, own_sem, send_sem, recv_sem, off_ssem, off_rsem, on_ssem, on_rsem, back_sem,
):
    tm = lax.axis_index("tm")
    fibre = lax.axis_index("fibre")
    core = fibre % 2
    hi = (fibre // 2) % 2
    count = 16
    flipped = tm + 1 - 2 * (tm % 2)
    partner = fibre + 1 - 2 * core
    outer = lax.rem(fibre + count - 1 + 2 * core, count)
    across = fibre + 2 - 4 * hi

    def there(tm_index, fibre_index):
        return {"fibre": fibre_index, "tm": tm_index}

    def chunk_of(step):
        return jnp.where(core == 0, step, CHUNKS - 1 - step)

    def x_copy(step):
        column = pl.multiple_of(chunk_of(step) * CHUNK, CHUNK)
        slot = step % 2
        return pltpu.make_async_copy(
            x_ref.at[:, :, pl.ds(column, CHUNK)], xb.at[slot], x_sem.at[slot]
        )

    def x_first(number):
        column = pl.multiple_of(chunk_of(0) * CHUNK, CHUNK)
        some = pl.ds(number * (BLOCK // 2), BLOCK // 2)
        return pltpu.make_async_copy(
            x_ref.at[some, :, pl.ds(column, CHUNK)], xb.at[0, some], x_sem.at[2 * number]
        )

    quarter = HALF // 2
    steer_copy = pltpu.make_async_copy(
        steer_ref.at[pl.ds(hi * HALF, HALF)], steer.at[pl.ds(0, HALF)], steer_sem.at[0]
    )
    steer_swap = pltpu.make_async_remote_copy(
        src_ref=steer_ref.at[pl.ds(hi * HALF + core * quarter, quarter)],
        dst_ref=steer.at[pl.ds(HALF + core * quarter, quarter)],
        send_sem=steer_sem.at[1],
        recv_sem=steer_sem.at[2],
        device_id=there(flipped, across),
        device_id_type=MESH,
    )

    def steer_share(who):
        part = steer.at[pl.ds(HALF + who * quarter, quarter)]
        return pltpu.make_async_remote_copy(
            src_ref=part,
            dst_ref=part,
            send_sem=steer_sem.at[3],
            recv_sem=steer_sem.at[4],
            device_id=there(tm, partner),
            device_id_type=MESH,
        )

    x_first(0).start()
    x_first(1).start()
    steer_copy.start()

    barrier = pltpu.get_barrier_semaphore()
    for index in range(len(OFFSETS)):
        pl.semaphore_signal(
            barrier, inc=1, device_id=there(peer(tm, core, index, 1), fibre), device_id_type=MESH
        )
    for other in (there(tm, partner), there(flipped, outer), there(flipped, across)):
        pl.semaphore_signal(barrier, inc=1, device_id=other, device_id_type=MESH)

    wide[...] = jnp.broadcast_to(taps_ref[...][:, :, None], (TAPS, NFFT, CHUNK))
    filt[:, SPAN * CHUNK :] = jnp.zeros((NFFT, CHUNK), bf16)
    recv[:, :, :, SPAN:] = jnp.zeros((CHUNKS, TM, 2, 1, 2 * HALF, CHUNK), bf16)

    whole = (0, SPAN)

    def piece(ref, step, device, part, frames):
        sets = pl.ds(0, 2) if part is None else pl.ds(part, 1)
        return ref.at[step, device, sets, pl.ds(frames[0], frames[1] - frames[0])]

    def to_peer(step, part, index, frames=whole):
        target = peer(tm, core, index, 1)
        slot = 0 if part is None else part
        return pltpu.make_async_remote_copy(
            src_ref=piece(send, step, target, part, frames),
            dst_ref=piece(recv, step, tm, part, frames),
            send_sem=send_sem.at[step, slot, index],
            recv_sem=recv_sem.at[step, slot, index],
            device_id=there(target, fibre),
            device_id_type=MESH,
        )

    def from_peer(step, part, index):
        source = peer(tm, core, index, -1)
        slot = 0 if part is None else part
        return pltpu.make_async_remote_copy(
            src_ref=piece(send, step, source, part, whole),
            dst_ref=piece(recv, step, source, part, whole),
            send_sem=send_sem.at[step, slot, index],
            recv_sem=recv_sem.at[step, slot, index],
            device_id=there(source, fibre),
            device_id_type=MESH,
        )

    def own_copy(step, part):
        return pltpu.make_async_copy(
            piece(send, step, tm, part, whole),
            piece(recv, step, tm, part, whole),
            own_sem.at[step, 0 if part is None else part],
        )

    def send_all(step, part):
        for index in range(len(OFFSETS)):
            to_peer(step, part, index).start()
        own_copy(step, part).start()

    def off_copy(aperture, part, landing):
        return pltpu.make_async_remote_copy(
            src_ref=off_out.at[aperture, part],
            dst_ref=off_in.at[aperture, landing],
            send_sem=off_ssem.at[aperture, part],
            recv_sem=off_rsem.at[aperture, landing],
            device_id=there(flipped, outer),
            device_id_type=MESH,
        )

    def on_copy(aperture, part):
        return pltpu.make_async_remote_copy(
            src_ref=on_out.at[aperture, part],
            dst_ref=on_in.at[aperture, part],
            send_sem=on_ssem.at[aperture, part],
            recv_sem=on_rsem.at[aperture, part],
            device_id=there(tm, partner),
            device_id_type=MESH,
        )

    back_copy = pltpu.make_async_remote_copy(
        src_ref=back_out,
        dst_ref=back_in,
        send_sem=back_sem.at[0],
        recv_sem=back_sem.at[1],
        device_id=there(flipped, fibre),
        device_id_type=MESH,
    )

    parts = [jnp.where(hi == h, 0, 1) for h in range(2)]
    targets = [[jnp.where(hi == h, t, t + 1 - 2 * (t % 2)) for h in range(2)] for t in range(TM)]

    def filter_frames(slot, frames):
        first_x, last_x = max(0, frames[0] - TAPS + 1), min(BLOCK, frames[1])

        def filter_rows(index, carry):
            rows = pl.ds(pl.multiple_of(index * 16, 16), 16)
            xs = {g: xb[slot, g, rows, :].astype(f32) for g in range(first_x, last_x)}
            ts = [wide[t, rows, :] for t in range(TAPS)]
            for frame in range(*frames):
                first, last = max(0, frame - BLOCK + 1), min(TAPS - 1, frame)
                total = ts[first] * xs[frame - first]
                for t in range(first + 1, last + 1):
                    total = total + ts[t] * xs[frame - t]
                filt[rows, frame * CHUNK : (frame + 1) * CHUNK] = total.astype(bf16)
            return carry

        lax.fori_loop(0, NFFT // 16, filter_rows, 0)

    def transform_frames(step, frames):
        def transform(pair, carry):
            columns = pl.ds(pl.multiple_of(pair * 2 * CHUNK, 2 * CHUNK), 2 * CHUNK)
            values = jnp.dot(
                fourier_ref[...], filt[:, columns], preferred_element_type=f32
            ).astype(bf16)
            for odd in range(2):
                for t in range(TM):
                    for h in range(2):
                        row = (2 * t + h) * 2 * HALF
                        send[step, targets[t][h], parts[h], pair * 2 + odd] = values[
                            row : row + 2 * HALF, odd * CHUNK : (odd + 1) * CHUNK
                        ]
            return carry

        lax.fori_loop(frames[0] // 2, (frames[1] + 1) // 2, transform, 0)

    for number, frames in enumerate(GROUPS):
        if number == 0 or number == 2:
            x_first(number // 2).wait()
        if number == 2:
            x_copy(1).start()
        filter_frames(0, frames)
        transform_frames(0, frames)
        if number == 0:
            pl.semaphore_wait(barrier, len(OFFSETS) + 3)
        for index in range(len(OFFSETS)):
            to_peer(0, None, index, frames).start()
        if number == 0:
            steer_swap.start()
    own_copy(0, None).start()

    def produce(step, carry):
        x_copy(step).wait()

        @pl.when(step < CHUNKS - 1)
        def _():
            x_copy(step + 1).start()

        filter_frames(step % 2, whole)
        transform_frames(step, whole)

        @pl.when(step == 1)
        def _():
            send_all(1, None)

        @pl.when(step > 1)
        def _():
            send_all(step, 1)

        @pl.when(step == 2)
        def _():
            send_all(2, 0)

        return carry

    lax.fori_loop(1, CHUNKS, produce, 0)
    send_all(3, 0)

    def arrive(step, part):
        for index in range(len(OFFSETS)):
            from_peer(step, part, index).wait_recv()
        own_copy(step, part).wait()

    def combine(step, part):
        columns = pl.ds(pl.multiple_of(chunk_of(step) * CHUNK, CHUNK), CHUNK)

        def block(i, carry):
            before = jnp.maximum(i - 1, 0)
            late = recv[step, before, part, pl.ds(BLOCK, BLOCK)].astype(f32)
            total = recv[step, i, part, pl.ds(0, BLOCK)].astype(f32) + jnp.where(i > 0, late, 0.0)
            turned = jnp.transpose(total, (1, 0, 2)).astype(bf16)
            for p in range(2):
                rows = pl.ds(pl.multiple_of(p * FRAMES + i * BLOCK, BLOCK), BLOCK)
                spec[pl.ds(part * HALF, HALF), rows, columns] = turned[p * HALF : (p + 1) * HALF]
            return carry

        lax.fori_loop(0, TM, block, 0)

    def product(k, u, width, m):
        if not isinstance(u, int):
            u, m = pl.multiple_of(u, CHUNK), pl.multiple_of(m, CHUNK)
        left = spec[k, :, pl.ds(u, width)]
        right = steer[k, :, pl.ds(m, width)]
        values = lax.dot_general(
            left, right, (((1,), (1,)), ((), ())), preferred_element_type=f32
        )
        real = values[:FRAMES, :SLOW] - values[FRAMES:, SLOW:]
        imag = values[FRAMES:, :SLOW] + values[:FRAMES, SLOW:]
        return real, imag

    def side(out, aperture, part, to_left, width):
        u = jnp.where(to_left, 0, 512 - width)
        m = jnp.where(to_left, APER - width, 0)

        def one(k, carry):
            real, imag = product(part * HALF + k, u, width, m)
            out[aperture, part, k, 0] = real.astype(bf16)
            out[aperture, part, k, 1] = imag.astype(bf16)
            return carry

        lax.fori_loop(0, HALF, one, 0)

    def off_near(part):
        side(off_out, core, part, core == 0, 128)
        off_copy(core, part, 1 - part).start()

    def off_far(part):
        side(off_out, 1 - core, part, core == 0, 384)
        off_copy(1 - core, part, 1 - part).start()

    def on_chip(part):
        side(on_out, 1 - core, part, core == 1, 128)
        on_copy(1 - core, part).start()
        side(on_out, core, part, core == 1, 384)
        on_copy(core, part).start()

    def own(part):
        def one(k, carry):
            k = part * HALF + k
            for aperture in range(2):
                real, imag = product(k, 0, 512, 384 - 256 * aperture)
                wide[k, pl.ds(aperture * 256, 128)] = real
                wide[k, pl.ds(aperture * 256 + 128, 128)] = imag
            return carry

        lax.fori_loop(0, HALF, one, 0)

    inside = jnp.logical_and(
        jnp.logical_or(fibre > 0, core == 1), jnp.logical_or(fibre < count - 1, core == 0)
    )

    def power(part, aperture, k):
        squares = []
        for piece in range(2):
            total = wide[part * HALF + k, pl.ds(aperture * 256 + piece * 128, 128)]
            total = total + on_in[aperture, part, k, piece].astype(f32)
            far = off_in[aperture, part, k, piece].astype(f32)
            total = total + jnp.where(inside, far, 0.0)
            squares.append(total * total)
        return squares[0] + squares[1]

    def wait_sides(part):
        for aperture in range(2):
            on_copy(aperture, part).wait_recv()
            off_copy(aperture, 1 - part, part).wait_recv()

    arrive(0, None)
    combine(0, 0)
    steer_copy.wait()
    off_near(0)
    combine(0, 1)
    steer_swap.wait()
    steer_share(core).start()
    arrive(1, None)
    combine(1, 1)
    combine(1, 0)
    steer_share(1 - core).wait_recv()
    off_near(1)
    arrive(2, 1)
    combine(2, 1)
    off_far(1)
    arrive(2, 0)
    combine(2, 0)
    off_far(0)
    arrive(3, 1)
    combine(3, 1)
    on_chip(1)
    own(1)
    wait_sides(1)

    def finish_other(k, carry):
        for aperture in range(2):
            back_out[aperture, k] = power(1, aperture, k).astype(bf16)
        return carry

    lax.fori_loop(0, HALF, finish_other, 0)
    back_copy.start()

    arrive(3, 0)
    combine(3, 0)
    on_chip(0)
    own(0)
    wait_sides(0)

    def finish_own(k, carry):
        for aperture in range(2):
            out_ref[aperture, hi * HALF + k] = power(0, aperture, k)
        return carry

    lax.fori_loop(0, HALF, finish_own, 0)

    back_copy.wait()

    def place(k, carry):
        for aperture in range(2):
            out_ref[aperture, (1 - hi) * HALF + k] = back_in[aperture, k].astype(f32)
        return carry

    lax.fori_loop(0, HALF, place, 0)

    steer_share(core).wait_send()
    for part in range(2):
        for aperture in range(2):
            on_copy(aperture, part).wait_send()
            off_copy(aperture, part, 1 - part).wait_send()

    def drain(index_of_parts, steps):
        def one(step, carry):
            for part in index_of_parts:
                for index in range(len(OFFSETS)):
                    to_peer(step, part, index).wait_send()
            return carry

        lax.fori_loop(*steps, one, 0)

    drain((None,), (0, 2))
    drain((0, 1), (2, CHUNKS))


def body(samples, filter_taps, steering):
    peers = len(OFFSETS)
    vmem = pl.BlockSpec(memory_space=pltpu.VMEM)
    hbm = pl.BlockSpec(memory_space=pl.ANY)
    dma = pltpu.SemaphoreType.DMA
    return pl.pallas_call(
        kernel,
        out_shape=pltpu.VMEM((2, BINS, FRAMES, SLOW), f32),
        in_specs=[hbm, vmem, vmem, hbm],
        out_specs=vmem,
        scratch_shapes=[
            pltpu.VMEM((2, BLOCK, NFFT, CHUNK), bf16),
            pltpu.VMEM((TAPS, NFFT, CHUNK), f32),
            pltpu.VMEM((NFFT, (SPAN + 1) * CHUNK), bf16),
            pltpu.VMEM((CHUNKS, TM, 2, SPAN + 1, 2 * HALF, CHUNK), bf16),
            pltpu.VMEM((CHUNKS, TM, 2, SPAN + 1, 2 * HALF, CHUNK), bf16),
            pltpu.VMEM((BINS, 2 * SLOW, APER), bf16),
            pltpu.VMEM((BINS, 2 * FRAMES, CHUNKS * CHUNK), bf16),
            pltpu.VMEM((2, 2, HALF, 2, FRAMES, SLOW), bf16),
            pltpu.VMEM((2, 2, HALF, 2, FRAMES, SLOW), bf16),
            pltpu.VMEM((2, 2, HALF, 2, FRAMES, SLOW), bf16),
            pltpu.VMEM((2, 2, HALF, 2, FRAMES, SLOW), bf16),
            pltpu.VMEM((2, HALF, FRAMES, SLOW), bf16),
            pltpu.VMEM((2, HALF, FRAMES, SLOW), bf16),
            dma((3,)),
            dma((5,)),
            dma((CHUNKS, 2)),
            dma((CHUNKS, 2, peers)),
            dma((CHUNKS, 2, peers)),
            dma((2, 2)),
            dma((2, 2)),
            dma((2, 2)),
            dma((2, 2)),
            dma((2,)),
        ],
        compiler_params=pltpu.CompilerParams(
            collective_id=0, has_side_effects=True, vmem_limit_bytes=60 * 2**20
        ),
        cost_estimate=pl.CostEstimate(
            flops=13 * 10**9, bytes_accessed=20 * 2**20, transcendentals=0
        ),
    )(
        samples.reshape(BLOCK, NFFT, samples.shape[1]),
        filter_taps,
        dft_table(),
        steering.reshape(BINS, 2 * SLOW, APER),
    )


def solution(mesh):
    in_specs = (P("tm", "fibre"), P(), P("tm", None, None, None))
    out_specs = P("fibre", "tm", None, None)
    return jax.shard_map(body, mesh=mesh, in_specs=in_specs, out_specs=out_specs, check_vma=False)
```

```python
import math

import jax
import jax.numpy as jnp
import numpy as np
from jax import lax
from jax.experimental import pallas as pl
from jax.experimental.pallas import tpu as pltpu
from jax.sharding import PartitionSpec as P

NFFT = 512
TAPS = 16
KB = 128
KLO = 64
APER = 1024
FRAMES = 128
SLOW = 128

BLOCK = 16
SPAN = 31
CHUNK = 128
CHUNKS = 4
TM = 8
BINS = 16
HALF = 8
GROUPS = ((0, 4), (4, 8), (8, 16), (16, 24), (24, 31))

MESH = pl.DeviceIdType.MESH
f32 = jnp.float32
bf16 = jnp.bfloat16

OFFSETS = ((2, 1), (0, 1), (2, 0), (1, 1), (1, 0), (3, 1), (3, 0))
OFFSETS1 = ((3, 0), (3, 1), (1, 0), (1, 1), (2, 0), (0, 1), (2, 1))


def dft_table():
    sample_index = np.arange(NFFT, dtype=np.int32)
    bin_index = np.arange(KB, dtype=np.int32) + KLO
    phases = (bin_index[:, None] * sample_index[None, :] % NFFT).astype(np.float32)
    phases = phases * np.float32(2.0 * math.pi / NFFT)
    fourier = np.stack([np.cos(phases), -np.sin(phases)], 0) / np.float32(math.sqrt(NFFT))
    fourier = fourier.reshape(2, TM, 2, HALF, NFFT).transpose(1, 2, 0, 3, 4)
    return jnp.asarray(fourier.reshape(2 * KB, NFFT), bf16)


def peer(tm, core, index, sign):
    (dy0, flip0), (dy1, flip1) = OFFSETS[index], OFFSETS1[index]
    dy, flip = jnp.where(core == 0, dy0, dy1), jnp.where(core == 0, flip0, flip1)
    lo = tm % 2
    y = lax.rem(tm // 2 + (dy if sign > 0 else 4 - dy), 4)
    return 2 * y + lo + flip - 2 * lo * flip


def kernel(
    x_ref, taps_ref, fourier_ref, steer_ref, out_ref,
    xb, wide, filt, send, recv, steer, spec, off_out, off_in, on_out, on_in, back_out, back_in,
    x_sem, steer_sem, own_sem, send_sem, recv_sem, off_ssem, off_rsem, on_ssem, on_rsem, back_sem,
):
    tm = lax.axis_index("tm")
    fibre = lax.axis_index("fibre")
    core = fibre % 2
    hi = (fibre // 2) % 2
    odd_x = (fibre // 4) % 2
    count = 16
    flipped = tm + 1 - 2 * (tm % 2)
    partner = fibre + 1 - 2 * core
    outer = lax.rem(fibre + count - 1 + 2 * core, count)
    across = fibre + 2 - 4 * hi
    beside = fibre + 4 - 8 * odd_x

    inside = jnp.logical_and(
        jnp.logical_or(fibre > 0, core == 1), jnp.logical_or(fibre < count - 1, core == 0)
    )

    def there(tm_index, fibre_index):
        return {"fibre": fibre_index, "tm": tm_index}

    def chunk_of(step):
        return jnp.where(core == 0, step, CHUNKS - 1 - step)

    def x_copy(step):
        column = pl.multiple_of(chunk_of(step) * CHUNK, CHUNK)
        slot = step % 2
        return pltpu.make_async_copy(
            x_ref.at[:, :, pl.ds(column, CHUNK)], xb.at[slot], x_sem.at[slot]
        )

    def x_first(number):
        column = pl.multiple_of(chunk_of(0) * CHUNK, CHUNK)
        some = pl.ds(number * (BLOCK // 2), BLOCK // 2)
        return pltpu.make_async_copy(
            x_ref.at[some, :, pl.ds(column, CHUNK)], xb.at[0, some], x_sem.at[2 * number]
        )

    quarter = HALF // 4
    steer_copy = pltpu.make_async_copy(
        steer_ref.at[pl.ds(hi * HALF, HALF)], steer.at[pl.ds(0, HALF)], steer_sem.at[0]
    )
    def quarter_of(parity, who):
        return parity * 2 * quarter + who * quarter

    steer_swap = pltpu.make_async_remote_copy(
        src_ref=steer_ref.at[pl.ds(hi * HALF + quarter_of(odd_x, core), quarter)],
        dst_ref=steer.at[pl.ds(HALF + quarter_of(odd_x, core), quarter)],
        send_sem=steer_sem.at[1],
        recv_sem=steer_sem.at[2],
        device_id=there(flipped, across),
        device_id_type=MESH,
    )

    def steer_pass(parity, who, sem, device):
        part = steer.at[pl.ds(HALF + quarter_of(parity, who), quarter)]
        return pltpu.make_async_remote_copy(
            src_ref=part,
            dst_ref=part,
            send_sem=steer_sem.at[sem],
            recv_sem=steer_sem.at[sem + 1],
            device_id=device,
            device_id_type=MESH,
        )

    def steer_beside(parity):
        return steer_pass(parity, core, 3, there(tm, beside))

    def steer_first(who):
        return steer_pass(odd_x, who, 5, there(tm, partner))

    def steer_second(who):
        return steer_pass(1 - odd_x, who, 7, there(tm, partner))

    x_first(0).start()
    x_first(1).start()
    steer_copy.start()

    barrier = pltpu.get_barrier_semaphore()
    for index in range(len(OFFSETS)):
        pl.semaphore_signal(
            barrier, inc=1, device_id=there(peer(tm, core, index, 1), fibre), device_id_type=MESH
        )
    others = (there(tm, partner), there(flipped, outer), there(flipped, across), there(tm, beside))
    for other in others:
        pl.semaphore_signal(barrier, inc=1, device_id=other, device_id_type=MESH)

    wide[...] = jnp.broadcast_to(taps_ref[...][:, :, None], (TAPS, NFFT, CHUNK))
    filt[:, SPAN * CHUNK :] = jnp.zeros((NFFT, CHUNK), bf16)
    @pl.when(jnp.logical_not(inside))
    def _():
        off_in[...] = jnp.zeros_like(off_in)

    recv[:, :, :, SPAN:] = jnp.zeros((CHUNKS, TM, 2, 1, 2 * HALF, CHUNK), bf16)

    whole = (0, SPAN)

    def piece(ref, step, device, part, frames):
        sets = pl.ds(0, 2) if part is None else pl.ds(part, 1)
        return ref.at[step, device, sets, pl.ds(frames[0], frames[1] - frames[0])]

    def to_peer(step, part, index, frames=whole):
        target = peer(tm, core, index, 1)
        slot = 0 if part is None else part
        return pltpu.make_async_remote_copy(
            src_ref=piece(send, step, target, part, frames),
            dst_ref=piece(recv, step, tm, part, frames),
            send_sem=send_sem.at[step, slot, index],
            recv_sem=recv_sem.at[step, slot, index],
            device_id=there(target, fibre),
            device_id_type=MESH,
        )

    def from_peer(step, part, index):
        source = peer(tm, core, index, -1)
        slot = 0 if part is None else part
        return pltpu.make_async_remote_copy(
            src_ref=piece(send, step, source, part, whole),
            dst_ref=piece(recv, step, source, part, whole),
            send_sem=send_sem.at[step, slot, index],
            recv_sem=recv_sem.at[step, slot, index],
            device_id=there(source, fibre),
            device_id_type=MESH,
        )

    def own_copy(step, part):
        return pltpu.make_async_copy(
            piece(send, step, tm, part, whole),
            piece(recv, step, tm, part, whole),
            own_sem.at[step, 0 if part is None else part],
        )

    def send_all(step, part):
        for index in range(len(OFFSETS)):
            to_peer(step, part, index).start()
        own_copy(step, part).start()

    def off_copy(aperture, part, landing):
        return pltpu.make_async_remote_copy(
            src_ref=off_out.at[aperture, part],
            dst_ref=off_in.at[aperture, landing],
            send_sem=off_ssem.at[aperture, part],
            recv_sem=off_rsem.at[aperture, landing],
            device_id=there(flipped, outer),
            device_id_type=MESH,
        )

    def on_copy(aperture, part):
        return pltpu.make_async_remote_copy(
            src_ref=on_out.at[aperture, part],
            dst_ref=on_in.at[aperture, part],
            send_sem=on_ssem.at[aperture, part],
            recv_sem=on_rsem.at[aperture, part],
            device_id=there(tm, partner),
            device_id_type=MESH,
        )

    back_copy = pltpu.make_async_remote_copy(
        src_ref=back_out,
        dst_ref=back_in,
        send_sem=back_sem.at[0],
        recv_sem=back_sem.at[1],
        device_id=there(flipped, fibre),
        device_id_type=MESH,
    )

    parts = [jnp.where(hi == h, 0, 1) for h in range(2)]
    targets = [[jnp.where(hi == h, t, t + 1 - 2 * (t % 2)) for h in range(2)] for t in range(TM)]

    def filter_frames(slot, frames):
        first_x, last_x = max(0, frames[0] - TAPS + 1), min(BLOCK, frames[1])

        def filter_rows(index, carry):
            rows = pl.ds(pl.multiple_of(index * 16, 16), 16)
            xs = {g: xb[slot, g, rows, :].astype(f32) for g in range(first_x, last_x)}
            ts = [wide[t, rows, :] for t in range(TAPS)]
            for frame in range(*frames):
                first, last = max(0, frame - BLOCK + 1), min(TAPS - 1, frame)
                total = ts[first] * xs[frame - first]
                for t in range(first + 1, last + 1):
                    total = total + ts[t] * xs[frame - t]
                filt[rows, frame * CHUNK : (frame + 1) * CHUNK] = total.astype(bf16)
            return carry

        lax.fori_loop(0, NFFT // 16, filter_rows, 0)

    def transform_frames(step, frames):
        def transform(pair, carry):
            columns = pl.ds(pl.multiple_of(pair * 2 * CHUNK, 2 * CHUNK), 2 * CHUNK)
            values = jnp.dot(
                fourier_ref[...], filt[:, columns], preferred_element_type=f32
            ).astype(bf16)
            for odd in range(2):
                for t in range(TM):
                    for h in range(2):
                        row = (2 * t + h) * 2 * HALF
                        send[step, targets[t][h], parts[h], pair * 2 + odd] = values[
                            row : row + 2 * HALF, odd * CHUNK : (odd + 1) * CHUNK
                        ]
            return carry

        lax.fori_loop(frames[0] // 2, (frames[1] + 1) // 2, transform, 0)

    for number, frames in enumerate(GROUPS):
        if number == 0 or number == 2:
            x_first(number // 2).wait()
        if number == 2:
            x_copy(1).start()
        filter_frames(0, frames)
        transform_frames(0, frames)
        if number == 0:
            pl.semaphore_wait(barrier, len(OFFSETS) + len(others))
        for index in range(len(OFFSETS)):
            to_peer(0, None, index, frames).start()
        if number == 0:
            steer_swap.start()
    own_copy(0, None).start()

    def produce(step, carry):
        x_copy(step).wait()

        @pl.when(step == 2)
        def _():
            steer_swap.wait_recv()
            steer_beside(odd_x).start()
            steer_first(core).start()

        @pl.when(step < CHUNKS - 1)
        def _():
            x_copy(step + 1).start()

        filter_frames(step % 2, whole)
        transform_frames(step, whole)

        @pl.when(step == 1)
        def _():
            send_all(1, None)

        @pl.when(step > 1)
        def _():
            send_all(step, 1)

        @pl.when(step == 2)
        def _():
            send_all(2, 0)

        return carry

    lax.fori_loop(1, CHUNKS, produce, 0)
    send_all(3, 0)

    def arrive(step, part):
        for index in range(len(OFFSETS)):
            from_peer(step, part, index).wait_recv()
        own_copy(step, part).wait()

    def combine(step, part):
        columns = pl.ds(pl.multiple_of(chunk_of(step) * CHUNK, CHUNK), CHUNK)

        def block(i, carry):
            before = jnp.maximum(i - 1, 0)
            late = recv[step, before, part, pl.ds(BLOCK, BLOCK)].astype(f32)
            total = recv[step, i, part, pl.ds(0, BLOCK)].astype(f32) + jnp.where(i > 0, late, 0.0)
            turned = jnp.transpose(total, (1, 0, 2)).astype(bf16)
            for p in range(2):
                rows = pl.ds(pl.multiple_of(p * FRAMES + i * BLOCK, BLOCK), BLOCK)
                spec[pl.ds(part * HALF, HALF), rows, columns] = turned[p * HALF : (p + 1) * HALF]
            return carry

        lax.fori_loop(0, TM, block, 0)

    def product(k, u, width, m):
        if not isinstance(u, int):
            u, m = pl.multiple_of(u, CHUNK), pl.multiple_of(m, CHUNK)
        left = spec[k, :, pl.ds(u, width)]
        right = steer[k, :, pl.ds(m, width)]
        values = lax.dot_general(
            left, right, (((1,), (1,)), ((), ())), preferred_element_type=f32
        )
        real = values[:FRAMES, :SLOW] - values[FRAMES:, SLOW:]
        imag = values[FRAMES:, :SLOW] + values[:FRAMES, SLOW:]
        return real, imag

    def side(out, aperture, part, to_left, width):
        u = jnp.where(to_left, 0, 512 - width)
        m = jnp.where(to_left, APER - width, 0)

        def one(k, carry):
            real, imag = product(part * HALF + k, u, width, m)
            out[aperture, part, k, 0] = real.astype(bf16)
            out[aperture, part, k, 1] = imag.astype(bf16)
            return carry

        lax.fori_loop(0, HALF, one, 0)

    def off_near(part):
        @pl.when(inside)
        def _():
            side(off_out, core, part, core == 0, 128)
            off_copy(core, part, 1 - part).start()

    def off_far(part):
        @pl.when(inside)
        def _():
            side(off_out, 1 - core, part, core == 0, 384)
            off_copy(1 - core, part, 1 - part).start()

    def on_chip(part):
        side(on_out, 1 - core, part, core == 1, 128)
        on_copy(1 - core, part).start()
        side(on_out, core, part, core == 1, 384)
        on_copy(core, part).start()

    def own(part):
        def one(k, carry):
            k = part * HALF + k
            for aperture in range(2):
                real, imag = product(k, 0, 512, 384 - 256 * aperture)
                wide[k, pl.ds(aperture * 256, 128)] = real
                wide[k, pl.ds(aperture * 256 + 128, 128)] = imag
            return carry

        lax.fori_loop(0, HALF, one, 0)

    def power(part, aperture, k):
        squares = []
        for piece in range(2):
            total = wide[part * HALF + k, pl.ds(aperture * 256 + piece * 128, 128)]
            total = total + on_in[aperture, part, k, piece].astype(f32)
            far = off_in[aperture, part, k, piece].astype(f32)
            total = total + jnp.where(inside, far, 0.0)
            squares.append(total * total)
        return squares[0] + squares[1]

    def wait_sides(part):
        for aperture in range(2):
            on_copy(aperture, part).wait_recv()

        @pl.when(inside)
        def _():
            for aperture in range(2):
                off_copy(aperture, 1 - part, part).wait_recv()

    arrive(0, None)
    combine(0, 0)
    steer_copy.wait()
    off_near(0)
    combine(0, 1)
    steer_beside(1 - odd_x).wait_recv()
    steer_second(core).start()
    arrive(1, None)
    combine(1, 1)
    combine(1, 0)
    steer_first(1 - core).wait_recv()
    steer_second(1 - core).wait_recv()
    off_near(1)
    arrive(2, 1)
    combine(2, 1)
    off_far(1)
    arrive(2, 0)
    combine(2, 0)
    off_far(0)
    arrive(3, 1)
    combine(3, 1)
    on_chip(1)
    own(1)
    wait_sides(1)

    def finish_other(k, carry):
        for aperture in range(2):
            back_out[aperture, k] = power(1, aperture, k).astype(bf16)
        return carry

    lax.fori_loop(0, HALF, finish_other, 0)
    back_copy.start()

    arrive(3, 0)
    combine(3, 0)
    on_chip(0)
    own(0)
    wait_sides(0)

    def finish_own(k, carry):
        for aperture in range(2):
            out_ref[aperture, hi * HALF + k] = power(0, aperture, k)
        return carry

    lax.fori_loop(0, HALF, finish_own, 0)

    back_copy.wait()

    def place(k, carry):
        for aperture in range(2):
            out_ref[aperture, (1 - hi) * HALF + k] = back_in[aperture, k].astype(f32)
        return carry

    lax.fori_loop(0, HALF, place, 0)

    steer_swap.wait_send()
    steer_beside(odd_x).wait_send()
    steer_first(core).wait_send()
    steer_second(core).wait_send()
    def drain_sides(part):
        for aperture in range(2):
            on_copy(aperture, part).wait_send()

        @pl.when(inside)
        def _():
            for aperture in range(2):
                off_copy(aperture, part, 1 - part).wait_send()

    drain_sides(0)
    drain_sides(1)

    def drain(index_of_parts, steps):
        def one(step, carry):
            for part in index_of_parts:
                for index in range(len(OFFSETS)):
                    to_peer(step, part, index).wait_send()
            return carry

        lax.fori_loop(*steps, one, 0)

    drain((None,), (0, 2))
    drain((0, 1), (2, CHUNKS))


def body(samples, filter_taps, steering):
    peers = len(OFFSETS)
    vmem = pl.BlockSpec(memory_space=pltpu.VMEM)
    hbm = pl.BlockSpec(memory_space=pl.ANY)
    dma = pltpu.SemaphoreType.DMA
    return pl.pallas_call(
        kernel,
        out_shape=pltpu.VMEM((2, BINS, FRAMES, SLOW), f32),
        in_specs=[hbm, vmem, vmem, hbm],
        out_specs=vmem,
        scratch_shapes=[
            pltpu.VMEM((2, BLOCK, NFFT, CHUNK), bf16),
            pltpu.VMEM((TAPS, NFFT, CHUNK), f32),
            pltpu.VMEM((NFFT, (SPAN + 1) * CHUNK), bf16),
            pltpu.VMEM((CHUNKS, TM, 2, SPAN + 1, 2 * HALF, CHUNK), bf16),
            pltpu.VMEM((CHUNKS, TM, 2, SPAN + 1, 2 * HALF, CHUNK), bf16),
            pltpu.VMEM((BINS, 2 * SLOW, APER), bf16),
            pltpu.VMEM((BINS, 2 * FRAMES, CHUNKS * CHUNK), bf16),
            pltpu.VMEM((2, 2, HALF, 2, FRAMES, SLOW), bf16),
            pltpu.VMEM((2, 2, HALF, 2, FRAMES, SLOW), bf16),
            pltpu.VMEM((2, 2, HALF, 2, FRAMES, SLOW), bf16),
            pltpu.VMEM((2, 2, HALF, 2, FRAMES, SLOW), bf16),
            pltpu.VMEM((2, HALF, FRAMES, SLOW), bf16),
            pltpu.VMEM((2, HALF, FRAMES, SLOW), bf16),
            dma((3,)),
            dma((9,)),
            dma((CHUNKS, 2)),
            dma((CHUNKS, 2, peers)),
            dma((CHUNKS, 2, peers)),
            dma((2, 2)),
            dma((2, 2)),
            dma((2, 2)),
            dma((2, 2)),
            dma((2,)),
        ],
        compiler_params=pltpu.CompilerParams(
            collective_id=0, has_side_effects=True, vmem_limit_bytes=60 * 2**20
        ),
        cost_estimate=pl.CostEstimate(
            flops=13 * 10**9, bytes_accessed=20 * 2**20, transcendentals=0
        ),
    )(
        samples.reshape(BLOCK, NFFT, samples.shape[1]),
        filter_taps,
        dft_table(),
        steering.reshape(BINS, 2 * SLOW, APER),
    )


def solution(mesh):
    in_specs = (P("tm", "fibre"), P(), P("tm", None, None, None))
    out_specs = P("fibre", "tm", None, None)
    return jax.shard_map(body, mesh=mesh, in_specs=in_specs, out_specs=out_specs, check_vma=False)
```

```python
import math

import jax
import jax.numpy as jnp
import numpy as np
from jax import lax
from jax.experimental import pallas as pl
from jax.experimental.pallas import tpu as pltpu
from jax.sharding import PartitionSpec as P

NFFT = 512
TAPS = 16
KB = 128
KLO = 64
APER = 1024
FRAMES = 128
SLOW = 128

BLOCK = 16
SPAN = 31
CHUNK = 128
CHUNKS = 4
TM = 8
BINS = 16
HALF = 8
GROUPS = ((0, 4), (4, 8), (8, 16), (16, 24), (24, 31))

MESH = pl.DeviceIdType.MESH
f32 = jnp.float32
bf16 = jnp.bfloat16

OFFSETS = ((2, 1), (0, 1), (2, 0), (1, 1), (1, 0), (3, 1), (3, 0))
OFFSETS1 = ((3, 0), (3, 1), (1, 0), (1, 1), (2, 0), (0, 1), (2, 1))


def dft_table():
    sample_index = np.arange(NFFT, dtype=np.int32)
    bin_index = np.arange(KB, dtype=np.int32) + KLO
    phases = (bin_index[:, None] * sample_index[None, :] % NFFT).astype(np.float32)
    phases = phases * np.float32(2.0 * math.pi / NFFT)
    fourier = np.stack([np.cos(phases), -np.sin(phases)], 0) / np.float32(math.sqrt(NFFT))
    fourier = fourier.reshape(2, TM, 2, HALF, NFFT).transpose(1, 2, 0, 3, 4)
    return jnp.asarray(fourier.reshape(2 * KB, NFFT), bf16)


def peer(tm, core, index, sign):
    (dy0, flip0), (dy1, flip1) = OFFSETS[index], OFFSETS1[index]
    dy, flip = jnp.where(core == 0, dy0, dy1), jnp.where(core == 0, flip0, flip1)
    lo = tm % 2
    y = lax.rem(tm // 2 + (dy if sign > 0 else 4 - dy), 4)
    return 2 * y + lo + flip - 2 * lo * flip


def kernel(
    x_ref, taps_ref, fourier_ref, steer_ref, out_ref,
    xb, wide, filt, send, recv, steer, spec, off_out, off_in, on_out, on_in, back_out, back_in,
    x_sem, steer_sem, own_sem, send_sem, recv_sem, off_ssem, off_rsem, on_ssem, on_rsem, back_sem,
):
    tm = lax.axis_index("tm")
    fibre = lax.axis_index("fibre")
    core = fibre % 2
    hi = (fibre // 2) % 2
    odd_x = (fibre // 4) % 2
    count = 16
    flipped = tm + 1 - 2 * (tm % 2)
    partner = fibre + 1 - 2 * core
    outer = lax.rem(fibre + count - 1 + 2 * core, count)
    across = fibre + 2 - 4 * hi
    beside = fibre + 4 - 8 * odd_x

    inside = jnp.logical_and(
        jnp.logical_or(fibre > 0, core == 1), jnp.logical_or(fibre < count - 1, core == 0)
    )

    def there(tm_index, fibre_index):
        return {"fibre": fibre_index, "tm": tm_index}

    def chunk_of(step):
        return jnp.where(core == 0, step, CHUNKS - 1 - step)

    def x_copy(step):
        column = pl.multiple_of(chunk_of(step) * CHUNK, CHUNK)
        slot = step % 2
        return pltpu.make_async_copy(
            x_ref.at[:, :, pl.ds(column, CHUNK)], xb.at[slot], x_sem.at[slot]
        )

    def x_first(number):
        column = pl.multiple_of(chunk_of(0) * CHUNK, CHUNK)
        some = pl.ds(number * (BLOCK // 2), BLOCK // 2)
        return pltpu.make_async_copy(
            x_ref.at[some, :, pl.ds(column, CHUNK)], xb.at[0, some], x_sem.at[2 * number]
        )

    quarter = HALF // 4
    steer_copy = pltpu.make_async_copy(
        steer_ref.at[pl.ds(hi * HALF, HALF)], steer.at[pl.ds(0, HALF)], steer_sem.at[0]
    )
    def quarter_of(parity, who):
        return parity * 2 * quarter + who * quarter

    steer_swap = pltpu.make_async_remote_copy(
        src_ref=steer_ref.at[pl.ds(hi * HALF + quarter_of(odd_x, core), quarter)],
        dst_ref=steer.at[pl.ds(HALF + quarter_of(odd_x, core), quarter)],
        send_sem=steer_sem.at[1],
        recv_sem=steer_sem.at[2],
        device_id=there(flipped, across),
        device_id_type=MESH,
    )

    def steer_pass(parity, who, sem, device):
        part = steer.at[pl.ds(HALF + quarter_of(parity, who), quarter)]
        return pltpu.make_async_remote_copy(
            src_ref=part,
            dst_ref=part,
            send_sem=steer_sem.at[sem],
            recv_sem=steer_sem.at[sem + 1],
            device_id=device,
            device_id_type=MESH,
        )

    def steer_beside(parity):
        return steer_pass(parity, core, 3, there(tm, beside))

    def steer_first(who):
        return steer_pass(odd_x, who, 5, there(tm, partner))

    def steer_second(who):
        return steer_pass(1 - odd_x, who, 7, there(tm, partner))

    x_first(0).start()
    x_first(1).start()
    steer_copy.start()

    barrier = pltpu.get_barrier_semaphore()
    for index in range(len(OFFSETS)):
        pl.semaphore_signal(
            barrier, inc=1, device_id=there(peer(tm, core, index, 1), fibre), device_id_type=MESH
        )
    others = (there(tm, partner), there(flipped, outer), there(flipped, across), there(tm, beside))
    for other in others:
        pl.semaphore_signal(barrier, inc=1, device_id=other, device_id_type=MESH)

    wide[...] = jnp.broadcast_to(taps_ref[...][:, :, None], (TAPS, NFFT, CHUNK))
    filt[:, SPAN * CHUNK :] = jnp.zeros((NFFT, CHUNK), bf16)
    @pl.when(jnp.logical_not(inside))
    def _():
        off_in[...] = jnp.zeros_like(off_in)

    recv[:, :, :, SPAN:] = jnp.zeros((CHUNKS, TM, 2, 1, 2 * HALF, CHUNK), bf16)

    whole = (0, SPAN)

    def piece(ref, step, device, part, frames):
        sets = pl.ds(0, 2) if part is None else pl.ds(part, 1)
        return ref.at[step, device, sets, pl.ds(frames[0], frames[1] - frames[0])]

    def to_peer(step, part, index, frames=whole):
        target = peer(tm, core, index, 1)
        slot = 0 if part is None else part
        return pltpu.make_async_remote_copy(
            src_ref=piece(send, step, target, part, frames),
            dst_ref=piece(recv, step, tm, part, frames),
            send_sem=send_sem.at[step, slot, index],
            recv_sem=recv_sem.at[step, slot, index],
            device_id=there(target, fibre),
            device_id_type=MESH,
        )

    def from_peer(step, part, index):
        source = peer(tm, core, index, -1)
        slot = 0 if part is None else part
        return pltpu.make_async_remote_copy(
            src_ref=piece(send, step, source, part, whole),
            dst_ref=piece(recv, step, source, part, whole),
            send_sem=send_sem.at[step, slot, index],
            recv_sem=recv_sem.at[step, slot, index],
            device_id=there(source, fibre),
            device_id_type=MESH,
        )

    def own_copy(step, part):
        return pltpu.make_async_copy(
            piece(send, step, tm, part, whole),
            piece(recv, step, tm, part, whole),
            own_sem.at[step, 0 if part is None else part],
        )

    def send_all(step, part):
        for index in range(len(OFFSETS)):
            to_peer(step, part, index).start()
        own_copy(step, part).start()

    def off_copy(aperture, part, landing):
        return pltpu.make_async_remote_copy(
            src_ref=off_out.at[aperture, part],
            dst_ref=off_in.at[aperture, landing],
            send_sem=off_ssem.at[aperture, part],
            recv_sem=off_rsem.at[aperture, landing],
            device_id=there(flipped, outer),
            device_id_type=MESH,
        )

    def on_copy(aperture, part):
        return pltpu.make_async_remote_copy(
            src_ref=on_out.at[aperture, part],
            dst_ref=on_in.at[aperture, part],
            send_sem=on_ssem.at[aperture, part],
            recv_sem=on_rsem.at[aperture, part],
            device_id=there(tm, partner),
            device_id_type=MESH,
        )

    def back_copy(aperture):
        return pltpu.make_async_remote_copy(
            src_ref=back_out.at[aperture],
            dst_ref=back_in.at[aperture],
            send_sem=back_sem.at[0, aperture],
            recv_sem=back_sem.at[1, aperture],
            device_id=there(flipped, fibre),
            device_id_type=MESH,
        )

    parts = [jnp.where(hi == h, 0, 1) for h in range(2)]
    targets = [[jnp.where(hi == h, t, t + 1 - 2 * (t % 2)) for h in range(2)] for t in range(TM)]

    def filter_frames(slot, frames):
        first_x, last_x = max(0, frames[0] - TAPS + 1), min(BLOCK, frames[1])

        def filter_rows(index, carry):
            rows = pl.ds(pl.multiple_of(index * 16, 16), 16)
            xs = {g: xb[slot, g, rows, :].astype(f32) for g in range(first_x, last_x)}
            ts = [wide[t, rows, :] for t in range(TAPS)]
            for frame in range(*frames):
                first, last = max(0, frame - BLOCK + 1), min(TAPS - 1, frame)
                total = ts[first] * xs[frame - first]
                for t in range(first + 1, last + 1):
                    total = total + ts[t] * xs[frame - t]
                filt[rows, frame * CHUNK : (frame + 1) * CHUNK] = total.astype(bf16)
            return carry

        lax.fori_loop(0, NFFT // 16, filter_rows, 0)

    def transform_frames(step, frames):
        def transform(pair, carry):
            columns = pl.ds(pl.multiple_of(pair * 2 * CHUNK, 2 * CHUNK), 2 * CHUNK)
            values = jnp.dot(
                fourier_ref[...], filt[:, columns], preferred_element_type=f32
            ).astype(bf16)
            for odd in range(2):
                for t in range(TM):
                    for h in range(2):
                        row = (2 * t + h) * 2 * HALF
                        send[step, targets[t][h], parts[h], pair * 2 + odd] = values[
                            row : row + 2 * HALF, odd * CHUNK : (odd + 1) * CHUNK
                        ]
            return carry

        lax.fori_loop(frames[0] // 2, (frames[1] + 1) // 2, transform, 0)

    for number, frames in enumerate(GROUPS):
        if number == 0 or number == 2:
            x_first(number // 2).wait()
        if number == 2:
            x_copy(1).start()
        filter_frames(0, frames)
        transform_frames(0, frames)
        if number == 0:
            pl.semaphore_wait(barrier, len(OFFSETS) + len(others))
        for index in range(len(OFFSETS)):
            to_peer(0, None, index, frames).start()
        if number == 0:
            steer_swap.start()
    own_copy(0, None).start()

    def produce(step, carry):
        x_copy(step).wait()

        @pl.when(step == 2)
        def _():
            steer_swap.wait_recv()
            steer_beside(odd_x).start()
            steer_first(core).start()

        @pl.when(step < CHUNKS - 1)
        def _():
            x_copy(step + 1).start()

        filter_frames(step % 2, whole)
        transform_frames(step, whole)

        @pl.when(step == 1)
        def _():
            send_all(1, None)

        @pl.when(step > 1)
        def _():
            send_all(step, 1)

        @pl.when(step == 2)
        def _():
            send_all(2, 0)

        return carry

    lax.fori_loop(1, CHUNKS, produce, 0)
    send_all(3, 0)

    def arrive(step, part):
        for index in range(len(OFFSETS)):
            from_peer(step, part, index).wait_recv()
        own_copy(step, part).wait()

    def combine(step, part):
        columns = pl.ds(pl.multiple_of(chunk_of(step) * CHUNK, CHUNK), CHUNK)

        def block(i, carry):
            before = jnp.maximum(i - 1, 0)
            late = recv[step, before, part, pl.ds(BLOCK, BLOCK)].astype(f32)
            total = recv[step, i, part, pl.ds(0, BLOCK)].astype(f32) + jnp.where(i > 0, late, 0.0)
            turned = jnp.transpose(total, (1, 0, 2)).astype(bf16)
            for p in range(2):
                rows = pl.ds(pl.multiple_of(p * FRAMES + i * BLOCK, BLOCK), BLOCK)
                spec[pl.ds(part * HALF, HALF), rows, columns] = turned[p * HALF : (p + 1) * HALF]
            return carry

        lax.fori_loop(0, TM, block, 0)

    def product(k, u, width, m):
        if not isinstance(u, int):
            u, m = pl.multiple_of(u, CHUNK), pl.multiple_of(m, CHUNK)
        left = spec[k, :, pl.ds(u, width)]
        right = steer[k, :, pl.ds(m, width)]
        values = lax.dot_general(
            left, right, (((1,), (1,)), ((), ())), preferred_element_type=f32
        )
        real = values[:FRAMES, :SLOW] - values[FRAMES:, SLOW:]
        imag = values[FRAMES:, :SLOW] + values[:FRAMES, SLOW:]
        return real, imag

    def side(out, aperture, part, to_left, width):
        u = jnp.where(to_left, 0, 512 - width)
        m = jnp.where(to_left, APER - width, 0)

        def one(k, carry):
            real, imag = product(part * HALF + k, u, width, m)
            out[aperture, part, k, 0] = real.astype(bf16)
            out[aperture, part, k, 1] = imag.astype(bf16)
            return carry

        lax.fori_loop(0, HALF, one, 0)

    def off_near(part):
        @pl.when(inside)
        def _():
            side(off_out, core, part, core == 0, 128)
            off_copy(core, part, 1 - part).start()

    def off_far(part):
        @pl.when(inside)
        def _():
            side(off_out, 1 - core, part, core == 0, 384)
            off_copy(1 - core, part, 1 - part).start()

    def on_chip(part):
        side(on_out, 1 - core, part, core == 1, 128)
        on_copy(1 - core, part).start()
        side(on_out, core, part, core == 1, 384)
        on_copy(core, part).start()

    def own(part):
        def one(k, carry):
            k = part * HALF + k
            for aperture in range(2):
                real, imag = product(k, 0, 512, 384 - 256 * aperture)
                wide[k, pl.ds(aperture * 256, 128)] = real
                wide[k, pl.ds(aperture * 256 + 128, 128)] = imag
            return carry

        lax.fori_loop(0, HALF, one, 0)

    def power(part, aperture, k):
        squares = []
        for piece in range(2):
            total = wide[part * HALF + k, pl.ds(aperture * 256 + piece * 128, 128)]
            total = total + on_in[aperture, part, k, piece].astype(f32)
            far = off_in[aperture, part, k, piece].astype(f32)
            total = total + jnp.where(inside, far, 0.0)
            squares.append(total * total)
        return squares[0] + squares[1]

    def wait_sides(part):
        for aperture in range(2):
            on_copy(aperture, part).wait_recv()

        @pl.when(inside)
        def _():
            for aperture in range(2):
                off_copy(aperture, 1 - part, part).wait_recv()

    arrive(0, None)
    combine(0, 0)
    steer_copy.wait()
    off_near(0)
    combine(0, 1)
    steer_beside(1 - odd_x).wait_recv()
    steer_second(core).start()
    arrive(1, None)
    combine(1, 1)
    combine(1, 0)
    steer_first(1 - core).wait_recv()
    steer_second(1 - core).wait_recv()
    off_near(1)
    arrive(2, 1)
    combine(2, 1)
    off_far(1)
    arrive(2, 0)
    combine(2, 0)
    off_far(0)
    arrive(3, 1)
    combine(3, 1)
    on_chip(1)
    own(1)
    wait_sides(1)

    for aperture in range(2):

        def finish_other(k, carry):
            back_out[aperture, k] = power(1, aperture, k).astype(bf16)
            return carry

        lax.fori_loop(0, HALF, finish_other, 0)
        back_copy(aperture).start()

    arrive(3, 0)
    combine(3, 0)
    on_chip(0)
    own(0)
    wait_sides(0)

    def finish_own(k, carry):
        for aperture in range(2):
            out_ref[aperture, hi * HALF + k] = power(0, aperture, k)
        return carry

    lax.fori_loop(0, HALF, finish_own, 0)

    for aperture in range(2):
        back_copy(aperture).wait()

        def place(k, carry):
            out_ref[aperture, (1 - hi) * HALF + k] = back_in[aperture, k].astype(f32)
            return carry

        lax.fori_loop(0, HALF, place, 0)

    steer_swap.wait_send()
    steer_beside(odd_x).wait_send()
    steer_first(core).wait_send()
    steer_second(core).wait_send()
    def drain_sides(part):
        for aperture in range(2):
            on_copy(aperture, part).wait_send()

        @pl.when(inside)
        def _():
            for aperture in range(2):
                off_copy(aperture, part, 1 - part).wait_send()

    drain_sides(0)
    drain_sides(1)

    def drain(index_of_parts, steps):
        def one(step, carry):
            for part in index_of_parts:
                for index in range(len(OFFSETS)):
                    to_peer(step, part, index).wait_send()
            return carry

        lax.fori_loop(*steps, one, 0)

    drain((None,), (0, 2))
    drain((0, 1), (2, CHUNKS))


def body(samples, filter_taps, steering):
    peers = len(OFFSETS)
    vmem = pl.BlockSpec(memory_space=pltpu.VMEM)
    hbm = pl.BlockSpec(memory_space=pl.ANY)
    dma = pltpu.SemaphoreType.DMA
    return pl.pallas_call(
        kernel,
        out_shape=pltpu.VMEM((2, BINS, FRAMES, SLOW), f32),
        in_specs=[hbm, vmem, vmem, hbm],
        out_specs=vmem,
        scratch_shapes=[
            pltpu.VMEM((2, BLOCK, NFFT, CHUNK), bf16),
            pltpu.VMEM((TAPS, NFFT, CHUNK), f32),
            pltpu.VMEM((NFFT, (SPAN + 1) * CHUNK), bf16),
            pltpu.VMEM((CHUNKS, TM, 2, SPAN + 1, 2 * HALF, CHUNK), bf16),
            pltpu.VMEM((CHUNKS, TM, 2, SPAN + 1, 2 * HALF, CHUNK), bf16),
            pltpu.VMEM((BINS, 2 * SLOW, APER), bf16),
            pltpu.VMEM((BINS, 2 * FRAMES, CHUNKS * CHUNK), bf16),
            pltpu.VMEM((2, 2, HALF, 2, FRAMES, SLOW), bf16),
            pltpu.VMEM((2, 2, HALF, 2, FRAMES, SLOW), bf16),
            pltpu.VMEM((2, 2, HALF, 2, FRAMES, SLOW), bf16),
            pltpu.VMEM((2, 2, HALF, 2, FRAMES, SLOW), bf16),
            pltpu.VMEM((2, HALF, FRAMES, SLOW), bf16),
            pltpu.VMEM((2, HALF, FRAMES, SLOW), bf16),
            dma((3,)),
            dma((9,)),
            dma((CHUNKS, 2)),
            dma((CHUNKS, 2, peers)),
            dma((CHUNKS, 2, peers)),
            dma((2, 2)),
            dma((2, 2)),
            dma((2, 2)),
            dma((2, 2)),
            dma((2, 2)),
        ],
        compiler_params=pltpu.CompilerParams(
            collective_id=0, has_side_effects=True, vmem_limit_bytes=60 * 2**20
        ),
        cost_estimate=pl.CostEstimate(
            flops=13 * 10**9, bytes_accessed=20 * 2**20, transcendentals=0
        ),
    )(
        samples.reshape(BLOCK, NFFT, samples.shape[1]),
        filter_taps,
        dft_table(),
        steering.reshape(BINS, 2 * SLOW, APER),
    )


def solution(mesh):
    in_specs = (P("tm", "fibre"), P(), P("tm", None, None, None))
    out_specs = P("fibre", "tm", None, None)
    return jax.shard_map(body, mesh=mesh, in_specs=in_specs, out_specs=out_specs, check_vma=False)
```

```python
import math

import jax
import jax.numpy as jnp
import numpy as np
from jax import lax
from jax.experimental import pallas as pl
from jax.experimental.pallas import tpu as pltpu
from jax.sharding import PartitionSpec as P

NFFT = 512
TAPS = 16
KB = 128
KLO = 64
APER = 1024
FRAMES = 128
SLOW = 128

BLOCK = 16
SPAN = 31
CHUNK = 128
CHUNKS = 4
TM = 8
BINS = 16
HALF = 8
GROUPS = ((0, 4), (4, 8), (8, 16), (16, 24), (24, 31))

MESH = pl.DeviceIdType.MESH
f32 = jnp.float32
bf16 = jnp.bfloat16

OFFSETS = ((2, 1), (0, 1), (1, 1), (2, 0), (1, 0), (3, 1), (3, 0))
OFFSETS1 = ((3, 0), (3, 1), (1, 0), (2, 0), (1, 1), (0, 1), (2, 1))


def dft_table():
    sample_index = np.arange(NFFT, dtype=np.int32)
    bin_index = np.arange(KB, dtype=np.int32) + KLO
    phases = (bin_index[:, None] * sample_index[None, :] % NFFT).astype(np.float32)
    phases = phases * np.float32(2.0 * math.pi / NFFT)
    fourier = np.stack([np.cos(phases), -np.sin(phases)], 0) / np.float32(math.sqrt(NFFT))
    fourier = fourier.reshape(2, TM, 2, HALF, NFFT).transpose(1, 2, 0, 3, 4)
    return jnp.asarray(fourier.reshape(2 * KB, NFFT), bf16)


def peer(tm, core, index, sign):
    (dy0, flip0), (dy1, flip1) = OFFSETS[index], OFFSETS1[index]
    dy, flip = jnp.where(core == 0, dy0, dy1), jnp.where(core == 0, flip0, flip1)
    lo = tm % 2
    y = lax.rem(tm // 2 + (dy if sign > 0 else 4 - dy), 4)
    return 2 * y + lo + flip - 2 * lo * flip


def kernel(
    x_ref, taps_ref, fourier_ref, steer_ref, out_ref,
    xb, wide, filt, send, recv, steer, spec, off_out, off_in, on_out, on_in, back_out, back_in,
    x_sem, steer_sem, own_sem, send_sem, recv_sem, off_ssem, off_rsem, on_ssem, on_rsem, back_sem,
):
    tm = lax.axis_index("tm")
    fibre = lax.axis_index("fibre")
    core = fibre % 2
    hi = (fibre // 2) % 2
    odd_x = (fibre // 4) % 2
    count = 16
    flipped = tm + 1 - 2 * (tm % 2)
    partner = fibre + 1 - 2 * core
    outer = lax.rem(fibre + count - 1 + 2 * core, count)
    across = fibre + 2 - 4 * hi
    beside = fibre + 4 - 8 * odd_x

    inside = jnp.logical_and(
        jnp.logical_or(fibre > 0, core == 1), jnp.logical_or(fibre < count - 1, core == 0)
    )

    def there(tm_index, fibre_index):
        return {"fibre": fibre_index, "tm": tm_index}

    def chunk_of(step):
        return jnp.where(core == 0, step, CHUNKS - 1 - step)

    def x_copy(step):
        column = pl.multiple_of(chunk_of(step) * CHUNK, CHUNK)
        slot = step % 2
        return pltpu.make_async_copy(
            x_ref.at[:, :, pl.ds(column, CHUNK)], xb.at[slot], x_sem.at[slot]
        )

    def x_first(number):
        column = pl.multiple_of(chunk_of(0) * CHUNK, CHUNK)
        some = pl.ds(number * (BLOCK // 2), BLOCK // 2)
        return pltpu.make_async_copy(
            x_ref.at[some, :, pl.ds(column, CHUNK)], xb.at[0, some], x_sem.at[2 * number]
        )

    quarter = HALF // 4
    steer_copy = pltpu.make_async_copy(
        steer_ref.at[pl.ds(hi * HALF, HALF)], steer.at[pl.ds(0, HALF)], steer_sem.at[0]
    )
    def quarter_of(parity, who):
        return parity * 2 * quarter + who * quarter

    steer_swap = pltpu.make_async_remote_copy(
        src_ref=steer_ref.at[pl.ds(hi * HALF + quarter_of(odd_x, core), quarter)],
        dst_ref=steer.at[pl.ds(HALF + quarter_of(odd_x, core), quarter)],
        send_sem=steer_sem.at[1],
        recv_sem=steer_sem.at[2],
        device_id=there(flipped, across),
        device_id_type=MESH,
    )

    def steer_pass(parity, who, sem, device):
        part = steer.at[pl.ds(HALF + quarter_of(parity, who), quarter)]
        return pltpu.make_async_remote_copy(
            src_ref=part,
            dst_ref=part,
            send_sem=steer_sem.at[sem],
            recv_sem=steer_sem.at[sem + 1],
            device_id=device,
            device_id_type=MESH,
        )

    def steer_beside(parity):
        return steer_pass(parity, core, 3, there(tm, beside))

    def steer_first(who):
        return steer_pass(odd_x, who, 5, there(tm, partner))

    def steer_second(who):
        return steer_pass(1 - odd_x, who, 7, there(tm, partner))

    x_first(0).start()
    x_first(1).start()
    steer_copy.start()

    barrier = pltpu.get_barrier_semaphore()
    for index in range(len(OFFSETS)):
        pl.semaphore_signal(
            barrier, inc=1, device_id=there(peer(tm, core, index, 1), fibre), device_id_type=MESH
        )
    others = (there(tm, partner), there(flipped, outer), there(flipped, across), there(tm, beside))
    for other in others:
        pl.semaphore_signal(barrier, inc=1, device_id=other, device_id_type=MESH)

    wide[...] = jnp.broadcast_to(taps_ref[...][:, :, None], (TAPS, NFFT, CHUNK))
    filt[:, SPAN * CHUNK :] = jnp.zeros((NFFT, CHUNK), bf16)
    @pl.when(jnp.logical_not(inside))
    def _():
        off_in[...] = jnp.zeros_like(off_in)

    recv[:, :, :, SPAN:] = jnp.zeros((CHUNKS, TM, 2, 1, 2 * HALF, CHUNK), bf16)

    whole = (0, SPAN)

    def piece(ref, step, device, part, frames):
        sets = pl.ds(0, 2) if part is None else pl.ds(part, 1)
        return ref.at[step, device, sets, pl.ds(frames[0], frames[1] - frames[0])]

    def to_peer(step, part, index, frames=whole):
        target = peer(tm, core, index, 1)
        slot = 0 if part is None else part
        return pltpu.make_async_remote_copy(
            src_ref=piece(send, step, target, part, frames),
            dst_ref=piece(recv, step, tm, part, frames),
            send_sem=send_sem.at[step, slot, index],
            recv_sem=recv_sem.at[step, slot, index],
            device_id=there(target, fibre),
            device_id_type=MESH,
        )

    def from_peer(step, part, index):
        source = peer(tm, core, index, -1)
        slot = 0 if part is None else part
        return pltpu.make_async_remote_copy(
            src_ref=piece(send, step, source, part, whole),
            dst_ref=piece(recv, step, source, part, whole),
            send_sem=send_sem.at[step, slot, index],
            recv_sem=recv_sem.at[step, slot, index],
            device_id=there(source, fibre),
            device_id_type=MESH,
        )

    def own_copy(step, part):
        return pltpu.make_async_copy(
            piece(send, step, tm, part, whole),
            piece(recv, step, tm, part, whole),
            own_sem.at[step, 0 if part is None else part],
        )

    def send_all(step, part):
        for index in range(len(OFFSETS)):
            to_peer(step, part, index).start()
        own_copy(step, part).start()

    def off_copy(aperture, part, landing):
        return pltpu.make_async_remote_copy(
            src_ref=off_out.at[aperture, part],
            dst_ref=off_in.at[aperture, landing],
            send_sem=off_ssem.at[aperture, part],
            recv_sem=off_rsem.at[aperture, landing],
            device_id=there(flipped, outer),
            device_id_type=MESH,
        )

    def on_copy(aperture, part):
        return pltpu.make_async_remote_copy(
            src_ref=on_out.at[aperture, part],
            dst_ref=on_in.at[aperture, part],
            send_sem=on_ssem.at[aperture, part],
            recv_sem=on_rsem.at[aperture, part],
            device_id=there(tm, partner),
            device_id_type=MESH,
        )

    back_copy = pltpu.make_async_remote_copy(
        src_ref=back_out,
        dst_ref=back_in,
        send_sem=back_sem.at[0],
        recv_sem=back_sem.at[1],
        device_id=there(flipped, fibre),
        device_id_type=MESH,
    )

    parts = [jnp.where(hi == h, 0, 1) for h in range(2)]
    targets = [[jnp.where(hi == h, t, t + 1 - 2 * (t % 2)) for h in range(2)] for t in range(TM)]

    def filter_frames(slot, frames):
        first_x, last_x = max(0, frames[0] - TAPS + 1), min(BLOCK, frames[1])

        def filter_rows(index, carry):
            rows = pl.ds(pl.multiple_of(index * 16, 16), 16)
            xs = {g: xb[slot, g, rows, :].astype(f32) for g in range(first_x, last_x)}
            ts = [wide[t, rows, :] for t in range(TAPS)]
            for frame in range(*frames):
                first, last = max(0, frame - BLOCK + 1), min(TAPS - 1, frame)
                total = ts[first] * xs[frame - first]
                for t in range(first + 1, last + 1):
                    total = total + ts[t] * xs[frame - t]
                filt[rows, frame * CHUNK : (frame + 1) * CHUNK] = total.astype(bf16)
            return carry

        lax.fori_loop(0, NFFT // 16, filter_rows, 0)

    def transform_frames(step, frames):
        def transform(pair, carry):
            columns = pl.ds(pl.multiple_of(pair * 2 * CHUNK, 2 * CHUNK), 2 * CHUNK)
            values = jnp.dot(
                fourier_ref[...], filt[:, columns], preferred_element_type=f32
            ).astype(bf16)
            for odd in range(2):
                for t in range(TM):
                    for h in range(2):
                        row = (2 * t + h) * 2 * HALF
                        send[step, targets[t][h], parts[h], pair * 2 + odd] = values[
                            row : row + 2 * HALF, odd * CHUNK : (odd + 1) * CHUNK
                        ]
            return carry

        lax.fori_loop(frames[0] // 2, (frames[1] + 1) // 2, transform, 0)

    for number, frames in enumerate(GROUPS):
        if number == 0 or number == 2:
            x_first(number // 2).wait()
        if number == 2:
            x_copy(1).start()
        filter_frames(0, frames)
        transform_frames(0, frames)
        if number == 0:
            pl.semaphore_wait(barrier, len(OFFSETS) + len(others))
        for index in range(len(OFFSETS)):
            to_peer(0, None, index, frames).start()
        if number == 0:
            steer_swap.start()
    own_copy(0, None).start()

    def produce(step, carry):
        x_copy(step).wait()

        @pl.when(step == 2)
        def _():
            steer_swap.wait_recv()
            steer_beside(odd_x).start()
            steer_first(core).start()

        @pl.when(step < CHUNKS - 1)
        def _():
            x_copy(step + 1).start()

        filter_frames(step % 2, whole)
        transform_frames(step, whole)

        @pl.when(step == 1)
        def _():
            send_all(1, None)

        @pl.when(step > 1)
        def _():
            send_all(step, 1)

        @pl.when(step == 2)
        def _():
            send_all(2, 0)

        return carry

    lax.fori_loop(1, CHUNKS, produce, 0)
    send_all(3, 0)

    def arrive(step, part):
        for index in range(len(OFFSETS)):
            from_peer(step, part, index).wait_recv()
        own_copy(step, part).wait()

    def combine(step, part):
        columns = pl.ds(pl.multiple_of(chunk_of(step) * CHUNK, CHUNK), CHUNK)

        def block(i, carry):
            before = jnp.maximum(i - 1, 0)
            late = recv[step, before, part, pl.ds(BLOCK, BLOCK)].astype(f32)
            total = recv[step, i, part, pl.ds(0, BLOCK)].astype(f32) + jnp.where(i > 0, late, 0.0)
            turned = jnp.transpose(total, (1, 0, 2)).astype(bf16)
            for p in range(2):
                rows = pl.ds(pl.multiple_of(p * FRAMES + i * BLOCK, BLOCK), BLOCK)
                spec[pl.ds(part * HALF, HALF), rows, columns] = turned[p * HALF : (p + 1) * HALF]
            return carry

        lax.fori_loop(0, TM, block, 0)

    def product(k, u, width, m):
        if not isinstance(u, int):
            u, m = pl.multiple_of(u, CHUNK), pl.multiple_of(m, CHUNK)
        left = spec[k, :, pl.ds(u, width)]
        right = steer[k, :, pl.ds(m, width)]
        values = lax.dot_general(
            left, right, (((1,), (1,)), ((), ())), preferred_element_type=f32
        )
        real = values[:FRAMES, :SLOW] - values[FRAMES:, SLOW:]
        imag = values[FRAMES:, :SLOW] + values[:FRAMES, SLOW:]
        return real, imag

    def side(out, aperture, part, to_left, width):
        u = jnp.where(to_left, 0, 512 - width)
        m = jnp.where(to_left, APER - width, 0)

        def one(k, carry):
            real, imag = product(part * HALF + k, u, width, m)
            out[aperture, part, k, 0] = real.astype(bf16)
            out[aperture, part, k, 1] = imag.astype(bf16)
            return carry

        lax.fori_loop(0, HALF, one, 0)

    def off_near(part):
        @pl.when(inside)
        def _():
            side(off_out, core, part, core == 0, 128)
            off_copy(core, part, 1 - part).start()

    def off_far(part):
        @pl.when(inside)
        def _():
            side(off_out, 1 - core, part, core == 0, 384)
            off_copy(1 - core, part, 1 - part).start()

    def on_chip(part):
        side(on_out, 1 - core, part, core == 1, 128)
        on_copy(1 - core, part).start()
        side(on_out, core, part, core == 1, 384)
        on_copy(core, part).start()

    def own(part):
        def one(k, carry):
            k = part * HALF + k
            for aperture in range(2):
                real, imag = product(k, 0, 512, 384 - 256 * aperture)
                wide[k, pl.ds(aperture * 256, 128)] = real
                wide[k, pl.ds(aperture * 256 + 128, 128)] = imag
            return carry

        lax.fori_loop(0, HALF, one, 0)

    def power(part, aperture, k):
        squares = []
        for piece in range(2):
            total = wide[part * HALF + k, pl.ds(aperture * 256 + piece * 128, 128)]
            total = total + on_in[aperture, part, k, piece].astype(f32)
            far = off_in[aperture, part, k, piece].astype(f32)
            total = total + jnp.where(inside, far, 0.0)
            squares.append(total * total)
        return squares[0] + squares[1]

    def wait_sides(part):
        for aperture in range(2):
            on_copy(aperture, part).wait_recv()

        @pl.when(inside)
        def _():
            for aperture in range(2):
                off_copy(aperture, 1 - part, part).wait_recv()

    arrive(0, None)
    combine(0, 0)
    steer_copy.wait()
    off_near(0)
    combine(0, 1)
    steer_beside(1 - odd_x).wait_recv()
    steer_second(core).start()
    arrive(1, None)
    combine(1, 1)
    combine(1, 0)
    steer_first(1 - core).wait_recv()
    steer_second(1 - core).wait_recv()
    off_near(1)
    arrive(2, 1)
    combine(2, 1)
    off_far(1)
    arrive(2, 0)
    combine(2, 0)
    off_far(0)
    arrive(3, 1)
    combine(3, 1)
    on_chip(1)
    own(1)
    wait_sides(1)

    def finish_other(k, carry):
        for aperture in range(2):
            back_out[aperture, k] = power(1, aperture, k).astype(bf16)
        return carry

    lax.fori_loop(0, HALF, finish_other, 0)
    back_copy.start()

    arrive(3, 0)
    combine(3, 0)
    on_chip(0)
    own(0)
    wait_sides(0)

    def finish_own(k, carry):
        for aperture in range(2):
            out_ref[aperture, hi * HALF + k] = power(0, aperture, k)
        return carry

    lax.fori_loop(0, HALF, finish_own, 0)

    back_copy.wait()

    def place(k, carry):
        for aperture in range(2):
            out_ref[aperture, (1 - hi) * HALF + k] = back_in[aperture, k].astype(f32)
        return carry

    lax.fori_loop(0, HALF, place, 0)

    steer_swap.wait_send()
    steer_beside(odd_x).wait_send()
    steer_first(core).wait_send()
    steer_second(core).wait_send()
    def drain_sides(part):
        for aperture in range(2):
            on_copy(aperture, part).wait_send()

        @pl.when(inside)
        def _():
            for aperture in range(2):
                off_copy(aperture, part, 1 - part).wait_send()

    drain_sides(0)
    drain_sides(1)

    def drain(index_of_parts, steps):
        def one(step, carry):
            for part in index_of_parts:
                for index in range(len(OFFSETS)):
                    to_peer(step, part, index).wait_send()
            return carry

        lax.fori_loop(*steps, one, 0)

    drain((None,), (0, 2))
    drain((0, 1), (2, CHUNKS))


def body(samples, filter_taps, steering):
    peers = len(OFFSETS)
    vmem = pl.BlockSpec(memory_space=pltpu.VMEM)
    hbm = pl.BlockSpec(memory_space=pl.ANY)
    dma = pltpu.SemaphoreType.DMA
    return pl.pallas_call(
        kernel,
        out_shape=pltpu.VMEM((2, BINS, FRAMES, SLOW), f32),
        in_specs=[hbm, vmem, vmem, hbm],
        out_specs=vmem,
        scratch_shapes=[
            pltpu.VMEM((2, BLOCK, NFFT, CHUNK), bf16),
            pltpu.VMEM((TAPS, NFFT, CHUNK), f32),
            pltpu.VMEM((NFFT, (SPAN + 1) * CHUNK), bf16),
            pltpu.VMEM((CHUNKS, TM, 2, SPAN + 1, 2 * HALF, CHUNK), bf16),
            pltpu.VMEM((CHUNKS, TM, 2, SPAN + 1, 2 * HALF, CHUNK), bf16),
            pltpu.VMEM((BINS, 2 * SLOW, APER), bf16),
            pltpu.VMEM((BINS, 2 * FRAMES, CHUNKS * CHUNK), bf16),
            pltpu.VMEM((2, 2, HALF, 2, FRAMES, SLOW), bf16),
            pltpu.VMEM((2, 2, HALF, 2, FRAMES, SLOW), bf16),
            pltpu.VMEM((2, 2, HALF, 2, FRAMES, SLOW), bf16),
            pltpu.VMEM((2, 2, HALF, 2, FRAMES, SLOW), bf16),
            pltpu.VMEM((2, HALF, FRAMES, SLOW), bf16),
            pltpu.VMEM((2, HALF, FRAMES, SLOW), bf16),
            dma((3,)),
            dma((9,)),
            dma((CHUNKS, 2)),
            dma((CHUNKS, 2, peers)),
            dma((CHUNKS, 2, peers)),
            dma((2, 2)),
            dma((2, 2)),
            dma((2, 2)),
            dma((2, 2)),
            dma((2,)),
        ],
        compiler_params=pltpu.CompilerParams(
            collective_id=0, has_side_effects=True, vmem_limit_bytes=60 * 2**20
        ),
        cost_estimate=pl.CostEstimate(
            flops=13 * 10**9, bytes_accessed=20 * 2**20, transcendentals=0
        ),
    )(
        samples.reshape(BLOCK, NFFT, samples.shape[1]),
        filter_taps,
        dft_table(),
        steering.reshape(BINS, 2 * SLOW, APER),
    )


def solution(mesh):
    in_specs = (P("tm", "fibre"), P(), P("tm", None, None, None))
    out_specs = P("fibre", "tm", None, None)
    return jax.shard_map(body, mesh=mesh, in_specs=in_specs, out_specs=out_specs, check_vma=False)
```
